32 devices in a mesh: section: 2 (over x), shard: 16 (over z, y, core).
Axes of the slice: x: 2, y: 2, z: 4, core: 2. Of those that a mesh axis runs over, the one named last changes fastest.
Arguments:
- boundary: bfloat16 [2, 2, 8192, 768], P('section', None, 'shard'), may hold values from -6 to 6
- ln1_gain: bfloat16 [2, 768], P('section', 'shard'), may hold values from 0.099609375 to 1.8984375
- ln1_bias: bfloat16 [2, 768], P('section', 'shard'), may hold values from -3 to 3
- w_qkv: bfloat16 [2, 768, 2304], P('section', 'shard'), may hold values from -0.21875 to 0.21875
- qv_bias: bfloat16 [2, 1536], P('section', 'shard'), may hold values from -3 to 3
- w_out: bfloat16 [2, 768, 768], P('section', 'shard'), may hold values from -3.5 to 3.5
- out_bias: bfloat16 [2, 768], P('section', 'shard'), may hold values from -3 to 3
- ln2_gain: bfloat16 [2, 768], P('section', 'shard'), may hold values from 0.099609375 to 1.8984375
- ln2_bias: bfloat16 [2, 768], P('section', 'shard'), may hold values from -3 to 3
- w_up: bfloat16 [2, 768, 3072], P('section', 'shard'), may hold values from -0.21875 to 0.21875
- up_bias: bfloat16 [2, 3072], P('section', 'shard'), may hold values from -3 to 3
- w_down: bfloat16 [2, 3072, 768], P('section', 'shard'), may hold values from -0.109375 to 0.109375
- down_bias: bfloat16 [2, 768], P('section', 'shard'), may hold values from -3 to 3
Outputs:
- section_outputs: bfloat16 [2, 2, 8192, 768], P('section', None, 'shard')
- section_grads: bfloat16 [2, 2, 8192, 768], P('section', None, 'shard')
- ln1_gain_grad: float32 [2, 768], P('section', 'shard')
- ln1_bias_grad: float32 [2, 768], P('section', 'shard')
- w_qkv_grad: float32 [2, 768, 2304], P('section', 'shard')
- qv_bias_grad: float32 [2, 1536], P('section', 'shard')
- w_out_grad: float32 [2, 768, 768], P('section', 'shard')
- out_bias_grad: float32 [2, 768], P('section', 'shard')
- ln2_gain_grad: float32 [2, 768], P('section', 'shard')
- ln2_bias_grad: float32 [2, 768], P('section', 'shard')
- w_up_grad: float32 [2, 768, 3072], P('section', 'shard')
- up_bias_grad: float32 [2, 3072], P('section', 'shard')
- w_down_grad: float32 [2, 3072, 768], P('section', 'shard')
- down_bias_grad: float32 [2, 768], P('section', 'shard')
The draws below stay inside these ranges and needn't reach their ends.
All inputs are finite; a program needn't handle non-finite values.
Results may differ from the reference program's by a relative error of at most 0.015.
Values may be sent and summed in bfloat16 or wider, within the bound.
No kernel may reach another device: no remote copies, remote signals or barrier semaphores. Data moves between devices by JAX's collectives and lax.ppermute only.
A program may use at most 192 MiB of HBM per device.

```python
import jax
import jax.numpy as jnp
from jax import lax

D = 768
FF = 3072
HEADS = 12
HEAD_DIM = 64
TOK_DEV = 512
MB = 2
TOKENS_MB = 8192
N_SHARD = 16


def raised(drawn, own_key, source, target, shards_of, factor):
    owner, partner = [(jnp.arange(drawn.shape[dim]) // (drawn.shape[dim] // shards_of)).reshape([-1 if axis == dim else 1 for axis in range(drawn.ndim)]) for dim in (source, target)]
    chosen = jax.random.permutation(own_key, shards_of)[partner]
    strong = (owner == chosen) | (owner == (partner + shards_of // 2) % shards_of)
    return jnp.where(strong, factor * drawn, drawn)


def block_levels(stream_key, extent, shards, least, high):
    def one(position, blocks):
        draws = jax.random.uniform(jax.random.fold_in(jax.random.fold_in(stream_key, 6), position), (blocks,), jnp.float32, least / len(shards), high / len(shards))
        return jnp.repeat(jnp.exp(draws), extent[position] // blocks).reshape((-1,) + (1,) * (len(extent) - position - 1))

    level = one(*shards[0])
    for cut in shards[1:]:
        level = level * one(*cut)
    return level


def gaussian(key, dims, spread, reach, shards=(), held_as=jnp.bfloat16):
    result = jax.random.normal(key, dims, jnp.float32) * spread
    if len(shards) > 0:
        result = block_levels(key, dims, shards, -0.22, 0.18) * result
    return jnp.clip(result, min=-reach, max=reach).astype(held_as)


def noise_with(rng, shape, spread, most, split, heavy, kind=jnp.bfloat16):
    result = spread * jax.random.normal(rng, shape, jnp.float32)
    if split:
        result = result * block_levels(rng, shape, split, -0.22, 0.18)
    return jnp.clip(raised(result, jax.random.fold_in(rng, 3), *heavy), -most, most).astype(kind)


def setup_inputs(seed: int = 0) -> dict:
    key_of = jax.random.split(jax.random.key(seed), 14)
    boundary = noise_with(key_of[0], (2, MB, TOKENS_MB, D), 1.0, 6.0, ((0, 2), (2, 16)), (2, 3, 16, 2.0))
    ln1_gain = jnp.clip(1.0 + 0.18 * jax.random.normal(key_of[1], (2, D), jnp.float32), 0.099609375, 1.8984375).astype(jnp.bfloat16)
    ln1_bias = gaussian(key_of[2], (2, D), 0.5, 3.0, ((0, 2), (1, 16)))
    w_qkv = gaussian(key_of[3], (2, D, 3 * D), D ** -0.5, 0.21875, ((0, 2), (1, 16)))
    qv_bias = gaussian(key_of[4], (2, 2 * D), 0.5, 3.0, ((0, 2), (1, 16)))
    w_out = gaussian(key_of[5], (2, D, D), (max(D // 256, 1)) ** -0.5, 3.5, ((0, 2), (1, 16)))
    out_bias = gaussian(key_of[6], (2, D), 0.5, 3.0, ((0, 2), (1, 16)))
    ln2_gain = jnp.clip(1.0 + 0.18 * jax.random.normal(key_of[7], (2, D), jnp.float32), 0.099609375, 1.8984375).astype(jnp.bfloat16)
    ln2_bias = gaussian(key_of[8], (2, D), 0.5, 3.0, ((0, 2), (1, 16)))
    w_up = gaussian(key_of[9], (2, D, FF), D ** -0.5, 0.21875, ((0, 2), (1, 16)))
    up_bias = gaussian(key_of[10], (2, FF), 0.5, 3.0, ((0, 2), (1, 16)))
    w_down = gaussian(key_of[11], (2, FF, D), FF ** -0.5, 0.109375, ((0, 2), (1, 16)))
    down_bias = gaussian(key_of[12], (2, D), 0.5, 3.0, ((0, 2), (1, 16)))
    return {"boundary": boundary, "ln1_gain": ln1_gain, "ln1_bias": ln1_bias, "w_qkv": w_qkv, "qv_bias": qv_bias, "w_out": w_out, "out_bias": out_bias, "ln2_gain": ln2_gain, "ln2_bias": ln2_bias, "w_up": w_up, "up_bias": up_bias, "w_down": w_down, "down_bias": down_bias}


@jax.custom_vjp
def low(v):
    return lax.optimization_barrier(v.astype(jnp.bfloat16)).astype(jnp.float32)

@jax.custom_vjp
def low_back(v):
    return v

def low_keep(v):
    return (low(v), None)

def low_pass(kept, grad):
    return (grad,)

def back_keep(v):
    return (v, None)

def back_low(kept, grad):
    return (low(grad),)
low.defvjp(low_keep, low_pass)
low_back.defvjp(back_keep, back_low)
HIGHEST_PRECISION = lax.Precision.HIGHEST

def norm_affine(values, gain, bias):
    row_mean = lax.optimization_barrier(jnp.mean(values, axis=-1, keepdims=True))
    centred = values - row_mean
    variance = lax.optimization_barrier(jnp.mean(centred * centred, axis=-1, keepdims=True))
    return centred * lax.rsqrt(variance + 1e-05) * gain + bias

def product(left, right):
    return jnp.einsum('...d,de->...e', left, right, precision=HIGHEST_PRECISION)

def attend_sequence(inputs):
    queries, key_rows, value_rows = inputs
    length = queries.shape[0]
    head_shape = (length, HEADS, HEAD_DIM)
    scores = jnp.einsum('qhd,khd->hqk', queries.reshape(head_shape), key_rows.reshape(head_shape), precision=HIGHEST_PRECISION) * HEAD_DIM ** (-0.5)
    scores = low_back(scores)
    positions = jnp.arange(length)
    allowed = positions[None, :] <= positions[:, None]
    scores = jnp.where(allowed[None], scores, -1e+30)
    weights = jax.nn.softmax(scores, axis=-1)
    attended = jnp.einsum('hqk,khd->qhd', low(weights), value_rows.reshape(head_shape), precision=HIGHEST_PRECISION)
    return attended.reshape(length, HEADS * HEAD_DIM)

def layer(hidden, params):
    ln1_gain, ln1_bias, w_qkv, qv_bias, w_out, out_bias, ln2_gain, ln2_bias, w_up, up_bias, w_down, down_bias = params
    normed = low(norm_affine(hidden, ln1_gain, ln1_bias))
    joined = product(normed, w_qkv)
    queries = low_back(low(joined[..., :D] + qv_bias[:D]))
    key_rows = low_back(low(joined[..., D:2 * D]))
    value_rows = low_back(low(joined[..., 2 * D:] + qv_bias[D:]))
    attended = lax.map(jax.checkpoint(attend_sequence), (queries, key_rows, value_rows))
    attended = low_back(low(attended))
    residual = hidden + low_back(product(attended, w_out)) + out_bias
    normed_two = low(norm_affine(residual, ln2_gain, ln2_bias))
    before = low_back(product(normed_two, w_up)) + up_bias
    activated = low(jax.nn.gelu(before))
    return residual + low_back(product(activated, w_down)) + down_bias

def section_one(hidden, params):
    return low_back(low(layer(hidden, params)))

def reference(boundary, ln1_gain, ln1_bias, w_qkv, qv_bias, w_out, out_bias, ln2_gain, ln2_bias, w_up, up_bias, w_down, down_bias):
    weights = [item.astype(jnp.float32) for item in (ln1_gain, ln1_bias, w_qkv, qv_bias, w_out, out_bias, ln2_gain, ln2_bias, w_up, up_bias, w_down, down_bias)]
    lower = [item[0] for item in weights]
    upper = [item[1] for item in weights]
    seq_shape = (MB * N_SHARD, TOK_DEV, D)
    inputs = boundary[0].astype(jnp.float32).reshape(seq_shape)
    cotangent = boundary[1].astype(jnp.float32).reshape(seq_shape)
    first_out, back_one = jax.vjp(section_one, inputs, lower)
    second_out, back_two = jax.vjp(layer, first_out, upper)
    grad_mid, grads_upper = back_two(cotangent)
    grad_in, grads_lower = back_one(grad_mid)
    full_shape = (MB, TOK_DEV * N_SHARD, D)
    section_outputs = jnp.stack([first_out.reshape(full_shape), second_out.reshape(full_shape)]).astype(jnp.bfloat16)
    section_grads = jnp.stack([grad_in.reshape(full_shape), grad_mid.reshape(full_shape)]).astype(jnp.bfloat16)
    gradients = [jnp.stack([lower_part, upper_part]) for lower_part, upper_part in zip(grads_lower, grads_upper)]
    return (section_outputs, section_grads, gradients[0], gradients[1], gradients[2], gradients[3], gradients[4], gradients[5], gradients[6], gradients[7], gradients[8], gradients[9], gradients[10], gradients[11])
```

```python
import jax
import jax.numpy as jnp
from jax import lax
from jax.sharding import PartitionSpec as P

D = 768
HEADS = 12
HEAD_DIM = 64


def from_behind(value, axis, steps):
    count = lax.axis_size(axis)
    first, last = (max(0, -steps), min(count, count - steps))
    return lax.ppermute(value, axis, [(source, source + steps) for source in range(first, last)])


def norm_affine(values, gain, bias):
    row_mean = jnp.mean(values, axis=-1, keepdims=True)
    centred = values - row_mean
    variance = jnp.mean(centred * centred, axis=-1, keepdims=True)
    return centred * lax.rsqrt(variance + 1e-05) * gain + bias


def key_mask(rows):
    query_pos = jnp.arange(rows)[:, None]
    key_pos = jnp.arange(rows)[None, :]
    return key_pos <= query_pos


def head_groups(matrix):
    return matrix.reshape(matrix.shape[0], HEADS // 2, 2 * HEAD_DIM).transpose(1, 0, 2)


def split_heads(block):
    return block.reshape(block.shape[0], 2, HEAD_DIM)


def ungroup(stacked):
    return stacked.transpose(1, 0, 2).reshape(stacked.shape[1], HEADS * HEAD_DIM)


def masked_scores(head_q, head_k, allowed):
    scores = jnp.einsum(
        "qhd,khd->hqk", head_q, head_k, preferred_element_type=jnp.float32
    ) * HEAD_DIM ** (-0.5)
    return jnp.where(allowed[None], scores, -1e30)


def attend_forward(queries, key_rows, value_rows):
    rows = queries.shape[0]
    allowed = key_mask(rows)

    def one_group(inputs):
        group_q, group_k, group_v = inputs
        scores = masked_scores(split_heads(group_q), split_heads(group_k), allowed)
        row_max = jnp.max(scores, axis=-1, keepdims=True)
        exponent = jnp.exp(scores - row_max)
        row_sum = jnp.sum(exponent, axis=-1, keepdims=True)
        weights = (exponent / row_sum).astype(jnp.bfloat16)
        attended = jnp.einsum(
            "hqk,khd->qhd", weights, split_heads(group_v), preferred_element_type=jnp.float32
        )
        return (attended.reshape(rows, 2 * HEAD_DIM), row_max + jnp.log(row_sum))

    attended, log_sums = lax.map(
        one_group, (head_groups(queries), head_groups(key_rows), head_groups(value_rows))
    )
    return (ungroup(attended), log_sums)


def attend_backward(queries, key_rows, value_rows, grad_attended, log_sums):
    rows = queries.shape[0]
    allowed = key_mask(rows)

    def one_group(inputs):
        group_q, group_k, group_v, group_g, group_lse = inputs
        head_q = split_heads(group_q)
        head_k = split_heads(group_k)
        head_g = split_heads(group_g)
        scores = masked_scores(head_q, head_k, allowed)
        weights = jnp.exp(scores - group_lse)
        grad_prob = jnp.einsum(
            "qhd,khd->hqk", head_g, split_heads(group_v), preferred_element_type=jnp.float32
        )
        centre = jnp.sum(weights * grad_prob, axis=-1, keepdims=True)
        grad_scores = (weights * (grad_prob - centre)).astype(jnp.bfloat16)
        grad_q = jnp.einsum(
            "hqk,khd->qhd", grad_scores, head_k, preferred_element_type=jnp.float32
        ) * HEAD_DIM ** (-0.5)
        grad_k = jnp.einsum(
            "hqk,qhd->khd", grad_scores, head_q, preferred_element_type=jnp.float32
        ) * HEAD_DIM ** (-0.5)
        grad_v = jnp.einsum(
            "hqk,qhd->khd", weights.astype(jnp.bfloat16), head_g, preferred_element_type=jnp.float32
        )
        return (
            grad_q.reshape(rows, 2 * HEAD_DIM),
            grad_k.reshape(rows, 2 * HEAD_DIM),
            grad_v.reshape(rows, 2 * HEAD_DIM),
        )

    grad_q, grad_k, grad_v = lax.map(
        one_group,
        (
            head_groups(queries),
            head_groups(key_rows),
            head_groups(value_rows),
            head_groups(grad_attended),
            log_sums,
        ),
    )
    return (ungroup(grad_q), ungroup(grad_k), ungroup(grad_v))


def forward_layer(hidden, weights):
    (
        ln1_gain,
        ln1_bias,
        w_qkv,
        qv_bias,
        w_out,
        out_bias,
        ln2_gain,
        ln2_bias,
        w_up,
        up_bias,
        w_down,
        down_bias,
    ) = weights
    h_float = hidden.astype(jnp.float32)
    normed = norm_affine(
        h_float, ln1_gain.astype(jnp.float32), ln1_bias.astype(jnp.float32)
    ).astype(jnp.bfloat16)
    joined = jnp.dot(normed, w_qkv, preferred_element_type=jnp.float32)
    bias_float = qv_bias.astype(jnp.float32)
    queries = (joined[:, :D] + bias_float[:D]).astype(jnp.bfloat16)
    key_rows = joined[:, D : 2 * D].astype(jnp.bfloat16)
    value_rows = (joined[:, 2 * D :] + bias_float[D:]).astype(jnp.bfloat16)
    attended, log_sums = attend_forward(queries, key_rows, value_rows)
    attended = attended.astype(jnp.bfloat16)
    residual = (
        h_float
        + jnp.dot(attended, w_out, preferred_element_type=jnp.float32)
        + out_bias.astype(jnp.float32)
    )
    normed_two = norm_affine(
        residual, ln2_gain.astype(jnp.float32), ln2_bias.astype(jnp.float32)
    ).astype(jnp.bfloat16)
    before = jnp.dot(normed_two, w_up, preferred_element_type=jnp.float32) + up_bias.astype(
        jnp.float32
    )
    activated = jax.nn.gelu(before).astype(jnp.bfloat16)
    layer_out = (
        residual
        + jnp.dot(activated, w_down, preferred_element_type=jnp.float32)
        + down_bias.astype(jnp.float32)
    )
    kept = (
        hidden,
        normed,
        queries,
        key_rows,
        value_rows,
        attended,
        log_sums,
        residual,
        normed_two,
        before,
        activated,
    )
    return (layer_out, kept)


def backward_layer(kept, grad_out, weights):
    (
        ln1_gain,
        ln1_bias,
        w_qkv,
        qv_bias,
        w_out,
        out_bias,
        ln2_gain,
        ln2_bias,
        w_up,
        up_bias,
        w_down,
        down_bias,
    ) = weights
    (
        hidden,
        normed,
        queries,
        key_rows,
        value_rows,
        attended,
        log_sums,
        residual,
        normed_two,
        before,
        activated,
    ) = kept
    down_bias_grad = jnp.sum(grad_out, axis=0)
    grad_low = grad_out.astype(jnp.bfloat16)
    w_down_grad = jnp.einsum("tf,td->fd", activated, grad_low, preferred_element_type=jnp.float32)
    grad_act = jnp.einsum("td,fd->tf", grad_low, w_down, preferred_element_type=jnp.float32)
    _, gelu_back = jax.vjp(jax.nn.gelu, before)
    (grad_before,) = gelu_back(grad_act)
    up_bias_grad = jnp.sum(grad_before, axis=0)
    before_low = grad_before.astype(jnp.bfloat16)
    w_up_grad = jnp.einsum("td,tf->df", normed_two, before_low, preferred_element_type=jnp.float32)
    grad_normed_two = jnp.einsum("tf,df->td", before_low, w_up, preferred_element_type=jnp.float32)
    _, norm_back_two = jax.vjp(
        norm_affine, residual, ln2_gain.astype(jnp.float32), ln2_bias.astype(jnp.float32)
    )
    grad_res_norm, ln2_gain_grad, ln2_bias_grad = norm_back_two(grad_normed_two)
    grad_residual = grad_out + grad_res_norm
    out_bias_grad = jnp.sum(grad_residual, axis=0)
    residual_low = grad_residual.astype(jnp.bfloat16)
    w_out_grad = jnp.einsum("td,te->de", attended, residual_low, preferred_element_type=jnp.float32)
    grad_attended = jnp.einsum(
        "te,de->td", residual_low, w_out, preferred_element_type=jnp.float32
    ).astype(jnp.bfloat16)
    grad_q, grad_keys, grad_values = attend_backward(
        queries, key_rows, value_rows, grad_attended, log_sums
    )
    key_low = grad_keys.astype(jnp.bfloat16)
    value_low = grad_values.astype(jnp.bfloat16)
    query_low = grad_q.astype(jnp.bfloat16)
    qv_bias_grad = jnp.concatenate(
        [
            jnp.sum(query_low.astype(jnp.float32), axis=0),
            jnp.sum(value_low.astype(jnp.float32), axis=0),
        ]
    )
    grad_joined = jnp.concatenate([query_low, key_low, value_low], axis=1)
    w_qkv_grad = jnp.einsum("td,te->de", normed, grad_joined, preferred_element_type=jnp.float32)
    grad_normed = jnp.einsum("te,de->td", grad_joined, w_qkv, preferred_element_type=jnp.float32)
    _, norm_back_one = jax.vjp(
        norm_affine,
        hidden.astype(jnp.float32),
        ln1_gain.astype(jnp.float32),
        ln1_bias.astype(jnp.float32),
    )
    grad_h_norm, ln1_gain_grad, ln1_bias_grad = norm_back_one(grad_normed)
    grad_hidden = grad_residual + grad_h_norm
    layer_grads = [
        ln1_gain_grad,
        ln1_bias_grad,
        w_qkv_grad,
        qv_bias_grad,
        w_out_grad,
        out_bias_grad,
        ln2_gain_grad,
        ln2_bias_grad,
        w_up_grad,
        up_bias_grad,
        w_down_grad,
        down_bias_grad,
    ]
    return (grad_hidden, layer_grads)


LOW = jnp.bfloat16
FLOAT = jnp.float32


def hop(value, axis, target):
    count = lax.axis_size(axis)
    return lax.ppermute(value, axis, [(source, target(source)) for source in range(count)])


def over_section(value):
    return hop(value, "section", lambda source: 1 - source)


def over_core(value):
    return hop(value, "shard", lambda source: source ^ 1)


def over_y(value):
    return hop(value, "shard", lambda source: source ^ 2)


def over_z(value, steps):
    count = lax.axis_size("shard")
    return hop(value, "shard", lambda source: (source + 4 * steps) % count)


def place(buffer, block, index, dim):
    starts = [0] * buffer.ndim
    starts[dim] = index
    return lax.dynamic_update_slice(buffer, block, starts)


def take(value, index, size, dim):
    return lax.dynamic_slice_in_dim(value, index * size, size, dim)


def place_of():
    shard = lax.axis_index("shard")
    return (lax.axis_index("section"), shard // 4, (shard // 2) % 2, shard % 2)


def spread_z(block):
    _, z, _, _ = place_of()
    count = lax.axis_size("shard") // 4
    buffer = jnp.zeros((count,) + block.shape, block.dtype)
    buffer = place(buffer, block[None], z, 0)
    for steps in range(1, count):
        arrived = over_z(block, steps)
        buffer = place(buffer, arrived[None], (z - steps) % count, 0)
    return buffer


def pair(own, arrived, index, dim):
    own, arrived = jnp.expand_dims(own, dim), jnp.expand_dims(arrived, dim)
    is_low = index == 0
    return jnp.concatenate(
        [jnp.where(is_low, own, arrived), jnp.where(is_low, arrived, own)], axis=dim
    )


def spread_y(blocks):
    _, _, y, _ = place_of()
    return pair(blocks, over_y(blocks), y, 1)


def spread_x(blocks):
    x, _, _, _ = place_of()
    dim = blocks.ndim - 1
    arrived = over_section(blocks)
    is_low = x == 0
    return jnp.concatenate(
        [jnp.where(is_low, blocks, arrived), jnp.where(is_low, arrived, blocks)], axis=dim
    )


def spread_core(blocks):
    _, _, _, core = place_of()
    return pair(blocks, over_core(blocks), core, 2)


def finish_gather(stacked, x_last):
    if x_last:
        stacked = spread_x(spread_y(stacked))
    else:
        stacked = spread_y(spread_x(stacked))
    stacked = spread_core(stacked)
    return stacked.reshape(-1, stacked.shape[-1])


def halves_of_both(shard):
    x, _, _, _ = place_of()
    half = shard.shape[1] // 2
    own = take(shard, x, half, 1)
    arrived = over_section(take(shard, 1 - x, half, 1))
    is_low = x == 0
    return (jnp.where(is_low, own, arrived), jnp.where(is_low, arrived, own))


def gather_vectors(packed):
    x, _, y, core = place_of()
    stacked = spread_z(packed)
    stacked = pair(stacked, over_y(stacked), y, 1)
    stacked = pair(stacked, over_core(stacked), core, 2)
    stacked = stacked.reshape((-1,) + packed.shape)
    arrived = over_section(stacked)
    return (jnp.where(x == 0, stacked, arrived), jnp.where(x == 0, arrived, stacked))


def reduce_core(total):
    _, _, _, core = place_of()
    sent = lax.dynamic_index_in_dim(total, 1 - core, 2, keepdims=False)
    kept = lax.dynamic_index_in_dim(total, core, 2, keepdims=False)
    return (kept.astype(FLOAT) + over_core(sent).astype(FLOAT)).astype(LOW)


def reduce_y(total):
    _, _, y, _ = place_of()
    sent = lax.dynamic_index_in_dim(total, 1 - y, 1, keepdims=False)
    kept = lax.dynamic_index_in_dim(total, y, 1, keepdims=False)
    return (kept.astype(FLOAT) + over_y(sent).astype(FLOAT)).astype(LOW)


def reduce_x(total):
    x, _, _, _ = place_of()
    dim = total.ndim - 1
    half = total.shape[dim] // 2
    sent = take(total, 1 - x, half, dim)
    kept = take(total, x, half, dim)
    return (kept.astype(FLOAT) + over_section(sent).astype(FLOAT)).astype(LOW)


def reduce_z(total):
    _, z, _, _ = place_of()
    count = total.shape[0]
    result = lax.dynamic_index_in_dim(total, z, 0, keepdims=False).astype(FLOAT)
    for steps in range(1, count):
        sent = lax.dynamic_index_in_dim(total, (z + steps) % count, 0, keepdims=False)
        result = result + over_z(sent, steps).astype(FLOAT)
    return result


def reduce_matrix(total, x_last):
    count = lax.axis_size("shard")
    columns = total.shape[1]
    if x_last is None:
        return total
    total = total.reshape(count // 4, 2, 2, total.shape[0] // count, columns)
    total = reduce_core(total)
    total = reduce_y(reduce_x(total)) if x_last else reduce_x(reduce_y(total))
    return reduce_z(total)


def join_halves(first_layer, second_layer):
    x, _, _, _ = place_of()
    is_low = x == 0
    kept = jnp.where(is_low, first_layer, second_layer)
    arrived = over_section(jnp.where(is_low, second_layer, first_layer).astype(LOW)).astype(FLOAT)
    return jnp.concatenate(
        [jnp.where(is_low, kept, arrived), jnp.where(is_low, arrived, kept)], axis=1
    )


def scatter_vectors(first_layer, second_layer):
    x, z, y, core = place_of()
    count = lax.axis_size("shard")
    is_low = x == 0
    kept = jnp.where(is_low, first_layer, second_layer)
    total = kept + over_section(jnp.where(is_low, second_layer, first_layer))
    total = total.reshape((count // 4, 2, 2) + total.shape[1:])
    sent = lax.dynamic_index_in_dim(total, 1 - core, 2, keepdims=False)
    total = lax.dynamic_index_in_dim(total, core, 2, keepdims=False) + over_core(sent)
    sent = lax.dynamic_index_in_dim(total, 1 - y, 1, keepdims=False)
    total = lax.dynamic_index_in_dim(total, y, 1, keepdims=False) + over_y(sent)
    return reduce_z(total)


def both_gathered(shard, x_last, direct):
    if direct:
        first, second = halves_of_both(shard)
        return [finish_gather(spread_z(item), x_last) for item in (first, second)]
    own = lax.all_gather(shard, "shard", axis=0, tiled=True)
    arrived = over_section(own)
    is_low = lax.axis_index("section") == 0
    return [jnp.where(is_low, own, arrived), jnp.where(is_low, arrived, own)]


def both_reduced(first, second, x_last, direct):
    if direct:
        return join_halves(reduce_matrix(first, x_last), reduce_matrix(second, x_last))
    is_low = lax.axis_index("section") == 0
    kept = jnp.where(is_low, first, second).astype(FLOAT)
    arrived = over_section(jnp.where(is_low, second, first)).astype(FLOAT)
    return lax.psum_scatter(kept + arrived, "shard", scatter_dimension=0, tiled=True)


def unpack_vectors(stacked):
    rows = stacked.shape[0]
    singles = [stacked[:, item].reshape(-1) for item in range(6)]
    return singles + [stacked[:, 6:8].reshape(-1), stacked[:, 8:12].reshape(-1)]


def pack_vectors(singles, pair_vector, quad_vector, count):
    parts = [item.reshape(count, 1, -1) for item in singles]
    parts.append(pair_vector.reshape(count, 2, -1))
    parts.append(quad_vector.reshape(count, 4, -1))
    return jnp.concatenate(parts, axis=1)


def on_device(
    boundary,
    ln1_gain,
    ln1_bias,
    w_qkv,
    qv_bias,
    w_out,
    out_bias,
    ln2_gain,
    ln2_bias,
    w_up,
    up_bias,
    w_down,
    down_bias,
):
    x = lax.axis_index("section")
    is_first = x == 0
    count = lax.axis_size("shard")
    direct = count <= 16
    packed = pack_vectors(
        [ln1_gain, ln1_bias, out_bias, ln2_gain, ln2_bias, down_bias], qv_bias, up_bias, 1
    )[0]
    other = over_section(jnp.where(is_first, boundary[0, 1], boundary[0, 0]))
    hidden = jnp.where(is_first, boundary[0, 0], other)
    cotangent = jnp.where(is_first, other, boundary[0, 1])
    vectors = gather_vectors(packed)
    qk_both = both_gathered(w_qkv[0, :, : 2 * D], True, direct)
    vo_both = both_gathered(jnp.concatenate([w_qkv[0, :, 2 * D :], w_out[0]], axis=1), False, direct)
    up_both = both_gathered(w_up[0], True, direct)
    down_both = both_gathered(w_down[0], False, direct)
    layers = []
    for index in range(2):
        singles = unpack_vectors(vectors[index])
        g1, b1, ob, g2, b2, db, qvb, ub = singles
        qkv = jnp.concatenate([qk_both[index], vo_both[index][:, :D]], axis=1)
        layers.append(
            (g1, b1, qkv, qvb, vo_both[index][:, D:], ob, g2, b2, up_both[index], ub, down_both[index], db)
        )
    first_out, kept_first = forward_layer(hidden, layers[0])
    first_low = first_out.astype(LOW)
    second_out, kept_second = forward_layer(first_low, layers[1])
    second_low = second_out.astype(LOW)
    grad_mid, grads_second = backward_layer(kept_second, cotangent.astype(FLOAT), layers[1])
    mid_low = grad_mid.astype(LOW)
    grad_in, grads_first = backward_layer(kept_first, mid_low.astype(FLOAT), layers[0])
    in_low = grad_in.astype(LOW)
    returned = over_section(jnp.stack([jnp.where(is_first, second_low, first_low), jnp.where(is_first, mid_low, in_low)]))
    own_out = jnp.where(is_first, first_low, second_low)
    own_grad = jnp.where(is_first, in_low, mid_low)
    section_outputs = jnp.where(is_first, jnp.stack([own_out, returned[0]]), jnp.stack([returned[0], own_out]))[None]
    section_grads = jnp.where(is_first, jnp.stack([own_grad, returned[1]]), jnp.stack([returned[1], own_grad]))[None]
    low_grads = []
    packed_grads = []
    for grads in (grads_first, grads_second):
        g1, b1, qkv, qvb, out, ob, g2, b2, up, ub, down, db = grads
        low_grads.append(
            (
                qkv[:, : 2 * D].astype(LOW),
                jnp.concatenate([qkv[:, 2 * D :], out], axis=1).astype(LOW),
                up.astype(LOW),
                down.astype(LOW),
            )
        )
        packed_grads.append(pack_vectors([g1, b1, ob, g2, b2, db], qvb, ub, count))
    x_orders = (True, False, True, False)
    qk, vo, up, down = [
        both_reduced(low_first, low_second, x_last, direct)
        for low_first, low_second, x_last in zip(low_grads[0], low_grads[1], x_orders)
    ]
    vector = scatter_vectors(packed_grads[0], packed_grads[1])
    return (
        section_outputs,
        section_grads,
        vector[0:1],
        vector[1:2],
        jnp.concatenate([qk, vo[:, :D]], axis=1)[None],
        vector[6:8].reshape(1, -1),
        vo[:, D:][None],
        vector[2:3],
        vector[3:4],
        vector[4:5],
        up[None],
        vector[8:12].reshape(1, -1),
        down[None],
        vector[5:6],
    )


def solution(mesh):
    placed = (
        P("section", None, "shard", None),
        P("section", "shard"),
        P("section", "shard"),
        P("section", "shard", None),
        P("section", "shard"),
        P("section", "shard", None),
        P("section", "shard"),
        P("section", "shard"),
        P("section", "shard"),
        P("section", "shard", None),
        P("section", "shard"),
        P("section", "shard", None),
        P("section", "shard"),
    )
    return jax.shard_map(
        on_device,
        mesh=mesh,
        in_specs=placed,
        out_specs=(
            P("section", None, "shard", None),
            P("section", None, "shard", None),
            P("section", "shard"),
            P("section", "shard"),
            P("section", "shard", None),
            P("section", "shard"),
            P("section", "shard", None),
            P("section", "shard"),
            P("section", "shard"),
            P("section", "shard"),
            P("section", "shard", None),
            P("section", "shard"),
            P("section", "shard", None),
            P("section", "shard"),
        ),
        check_vma=False,
    )
```

```python
import jax
import jax.numpy as jnp
from jax import lax
from jax.experimental import pallas as pl
from jax.experimental.pallas import tpu as pltpu
from jax.sharding import PartitionSpec as P

D = 768
LOW = jnp.bfloat16
FLOAT = jnp.float32
CHUNK = 256


def norm_affine(values, gain, bias):
    row_mean = jnp.mean(values, axis=-1, keepdims=True)
    centred = values - row_mean
    variance = jnp.mean(centred * centred, axis=-1, keepdims=True)
    return centred * lax.rsqrt(variance + 1e-05) * gain + bias


def dot_nt(a,b):
    return lax.dot_general(a,b,(((1,),(1,)),((),())),preferred_element_type=FLOAT)


def dot_nn(a,b):
    return lax.dot_general(a,b,(((1,),(0,)),((),())),preferred_element_type=FLOAT)


def dot_tn(a,b):
    return lax.dot_general(a,b,(((0,),(0,)),((),())),preferred_element_type=FLOAT)


def head_part(block, head):
    lane = lax.broadcasted_iota(jnp.int32, block.shape, 1)
    return jnp.where((lane >= 64) == (head == 1), block, jnp.zeros_like(block))


def probabilities(q_rows, k_rows, first):
    scores = dot_nt(q_rows, k_rows)
    row = lax.broadcasted_iota(jnp.int32, scores.shape, 0) + first
    col = lax.broadcasted_iota(jnp.int32, scores.shape, 1)
    scores = jnp.where(col <= row, scores, -1e30)
    top = jnp.max(scores, axis=-1, keepdims=True)
    exponent = jnp.exp(scores - top)
    return exponent * (1.0 / jnp.sum(exponent, axis=-1, keepdims=True))


def fwd_kernel(q_ref, k_ref, v_ref, o_ref):
    rows = q_ref.shape[0]
    k = k_ref[...]; v = v_ref[...]
    for first in range(0, rows, CHUNK):
        last = first + CHUNK
        q = q_ref[first:last, :] * LOW(0.125)
        total = None
        for head in range(2):
            p = probabilities(head_part(q, head), k[:last], first).astype(LOW)
            part = dot_nn(p, head_part(v[:last], head))
            total = part if total is None else total + part
        o_ref[first:last, :] = total.astype(LOW)


def attention_forward(qk, values):
    rows = qk.shape[0]
    pairs = D // 128
    first = pl.BlockSpec((rows, 128), lambda pair: (0, pair))
    second = pl.BlockSpec((rows, 128), lambda pair: (0, pair + pairs))
    return pl.pallas_call(
        fwd_kernel,
        grid=(pairs,),
        in_specs=[first, second, first],
        out_specs=first,
        out_shape=jax.ShapeDtypeStruct((rows, D), LOW),
        compiler_params=pltpu.CompilerParams(vmem_limit_bytes=32 * 1024 * 1024),
        cost_estimate=pl.CostEstimate(
            flops=40 * rows * rows * D, bytes_accessed=8 * rows * D, transcendentals=12 * rows * rows
        ),
        name="attend_forward",
    )(qk, qk, values)


def bwd_kernel(q_ref, k_ref, v_ref, g_ref, qk_out, v_out, dk_acc, dv_acc):
    rows = q_ref.shape[0]
    h = pl.program_id(0)
    k = k_ref[...]; v = v_ref[...]
    dk_acc[...] = jnp.zeros_like(dk_acc)
    dv_acc[...] = jnp.zeros_like(dv_acc)
    col = pl.multiple_of(h * 128, 128)
    for first in range(0, rows, CHUNK):
        last = first + CHUNK
        q = q_ref[first:last, :] * LOW(0.125)
        g = g_ref[first:last, :]
        dq = None
        for head in range(2):
            qh = head_part(q, head); gh = head_part(g, head)
            p = probabilities(qh, k[:last], first)
            dp = dot_nt(gh, v[:last])
            centre = jnp.sum(p * dp, axis=-1, keepdims=True)
            ds = (p * (dp - centre)).astype(LOW)
            part = dot_nn(ds, head_part(k[:last], head))
            dq = part if dq is None else dq + part
            dk_acc[:last, :] += dot_tn(ds, qh)
            dv_acc[:last, :] += dot_tn(p.astype(LOW), gh)
        qk_out[first:last, pl.ds(col, 128)] = (dq * 0.125).astype(LOW)
    qk_out[:, pl.ds(D + col, 128)] = dk_acc[...].astype(LOW)
    v_out[...] = dv_acc[...].astype(LOW)


def attention_backward(qk, values, grad):
    rows = qk.shape[0]
    pairs = D // 128
    first = pl.BlockSpec((rows, 128), lambda pair: (0, pair))
    second = pl.BlockSpec((rows, 128), lambda pair: (0, pair + pairs))
    return pl.pallas_call(
        bwd_kernel,
        grid=(pairs,),
        in_specs=[first, second, first, first],
        out_specs=[pl.BlockSpec((rows, 2 * D), lambda pair: (0, 0)), first],
        out_shape=[
            jax.ShapeDtypeStruct((rows, 2 * D), LOW),
            jax.ShapeDtypeStruct((rows, D), LOW),
        ],
        scratch_shapes=[pltpu.VMEM((rows, 128), FLOAT), pltpu.VMEM((rows, 128), FLOAT)],
        compiler_params=pltpu.CompilerParams(vmem_limit_bytes=32 * 1024 * 1024),
        cost_estimate=pl.CostEstimate(
            flops=80 * rows * rows * D, bytes_accessed=14 * rows * D, transcendentals=12 * rows * rows
        ),
        name="attend_backward",
    )(qk, qk, values, grad)


def hop(value, axis, target):
    count = lax.axis_size(axis)
    return lax.ppermute(value, axis, [(source, target(source)) for source in range(count)])


def over_section(value):
    return hop(value, "section", lambda source: 1 - source)


def over_core(value):
    return hop(value, "shard", lambda source: source ^ 1)


def over_y(value):
    return hop(value, "shard", lambda source: source ^ 2)


def over_z(value, steps):
    count = lax.axis_size("shard")
    return hop(value, "shard", lambda source: (source + 4 * steps) % count)


def place(buffer, block, index, dim):
    starts = [0] * buffer.ndim
    starts[dim] = index
    return lax.dynamic_update_slice(buffer, block, starts)


def take(value, index, size, dim):
    return lax.dynamic_slice_in_dim(value, index * size, size, dim)


def place_of():
    shard = lax.axis_index("shard")
    return (lax.axis_index("section"), shard // 4, (shard // 2) % 2, shard % 2)


def spread_z(block):
    _, z, _, _ = place_of()
    count = lax.axis_size("shard") // 4
    buffer = jnp.zeros((count,) + block.shape, block.dtype)
    buffer = place(buffer, block[None], z, 0)
    for steps in range(1, count):
        arrived = over_z(block, steps)
        buffer = place(buffer, arrived[None], (z - steps) % count, 0)
    return buffer


def pair(own, arrived, index, dim):
    own, arrived = jnp.expand_dims(own, dim), jnp.expand_dims(arrived, dim)
    is_low = index == 0
    return jnp.concatenate(
        [jnp.where(is_low, own, arrived), jnp.where(is_low, arrived, own)], axis=dim
    )


def spread_y(blocks):
    _, _, y, _ = place_of()
    return pair(blocks, over_y(blocks), y, 1)


def spread_x(blocks):
    x, _, _, _ = place_of()
    dim = blocks.ndim - 1
    arrived = over_section(blocks)
    is_low = x == 0
    return jnp.concatenate(
        [jnp.where(is_low, blocks, arrived), jnp.where(is_low, arrived, blocks)], axis=dim
    )


def spread_core(blocks):
    _, _, _, core = place_of()
    return pair(blocks, over_core(blocks), core, 2)


def halves_of_both(shard):
    x, _, _, _ = place_of()
    half = shard.shape[1] // 2
    own = take(shard, x, half, 1)
    arrived = over_section(take(shard, 1 - x, half, 1))
    is_low = x == 0
    return (jnp.where(is_low, own, arrived), jnp.where(is_low, arrived, own))


def gather_vectors(packed):
    x, _, y, core = place_of()
    stacked = spread_z(packed)
    stacked = pair(stacked, over_y(stacked), y, 1)
    stacked = pair(stacked, over_core(stacked), core, 2)
    stacked = stacked.reshape((-1,) + packed.shape)
    arrived = over_section(stacked)
    return (jnp.where(x == 0, stacked, arrived), jnp.where(x == 0, arrived, stacked))


def reduce_core(total):
    _, _, _, core = place_of()
    sent = lax.dynamic_index_in_dim(total, 1 - core, 2, keepdims=False)
    kept = lax.dynamic_index_in_dim(total, core, 2, keepdims=False)
    return (kept.astype(FLOAT) + over_core(sent).astype(FLOAT)).astype(LOW)


def reduce_y(total):
    _, _, y, _ = place_of()
    sent = lax.dynamic_index_in_dim(total, 1 - y, 1, keepdims=False)
    kept = lax.dynamic_index_in_dim(total, y, 1, keepdims=False)
    return (kept.astype(FLOAT) + over_y(sent).astype(FLOAT)).astype(LOW)


def reduce_x(total):
    x, _, _, _ = place_of()
    dim = total.ndim - 1
    half = total.shape[dim] // 2
    sent = take(total, 1 - x, half, dim)
    kept = take(total, x, half, dim)
    return (kept.astype(FLOAT) + over_section(sent).astype(FLOAT)).astype(LOW)


def reduce_z(total):
    _, z, _, _ = place_of()
    count = total.shape[0]
    result = lax.dynamic_index_in_dim(total, z, 0, keepdims=False).astype(FLOAT)
    for steps in range(1, count):
        sent = lax.dynamic_index_in_dim(total, (z + steps) % count, 0, keepdims=False)
        result = result + over_z(sent, steps).astype(FLOAT)
    return result


def join_halves(first_layer, second_layer):
    x, _, _, _ = place_of()
    is_low = x == 0
    kept = jnp.where(is_low, first_layer, second_layer)
    arrived = over_section(jnp.where(is_low, second_layer, first_layer).astype(LOW)).astype(FLOAT)
    return jnp.concatenate(
        [jnp.where(is_low, kept, arrived), jnp.where(is_low, arrived, kept)], axis=1
    )


def scatter_vectors(first_layer, second_layer):
    x, z, y, core = place_of()
    count = lax.axis_size("shard")
    is_low = x == 0
    kept = jnp.where(is_low, first_layer, second_layer)
    total = kept + over_section(jnp.where(is_low, second_layer, first_layer))
    total = total.reshape((count // 4, 2, 2) + total.shape[1:])
    sent = lax.dynamic_index_in_dim(total, 1 - core, 2, keepdims=False)
    total = lax.dynamic_index_in_dim(total, core, 2, keepdims=False) + over_core(sent)
    sent = lax.dynamic_index_in_dim(total, 1 - y, 1, keepdims=False)
    total = lax.dynamic_index_in_dim(total, y, 1, keepdims=False) + over_y(sent)
    return reduce_z(total)


def unpack_vectors(stacked):
    rows = stacked.shape[0]
    singles = [stacked[:, item].reshape(-1) for item in range(6)]
    return singles + [stacked[:, 6:8].reshape(-1), stacked[:, 8:12].reshape(-1)]


def pack_vectors(singles, pair_vector, quad_vector, count):
    parts = [item.reshape(count, 1, -1) for item in singles]
    parts.append(pair_vector.reshape(count, 2, -1))
    parts.append(quad_vector.reshape(count, 4, -1))
    return jnp.concatenate(parts, axis=1)


def tie(*values):
    return lax.optimization_barrier(values)


def second_stage(stacked, x_last):
    return spread_y(stacked) if x_last else spread_x(stacked)


def third_stage(stacked, x_last):
    return spread_x(stacked) if x_last else spread_y(stacked)


def core_stage(stacked):
    stacked = spread_core(stacked)
    return stacked.reshape(-1, stacked.shape[-1])


def core_reduced(total):
    count = lax.axis_size("shard")
    return reduce_core(
        total.reshape(count // 4, 2, 2, total.shape[0] // count, total.shape[1])
    )


def wide_reduced(total, x_last):
    return reduce_x(total) if x_last else reduce_y(total)


def narrow_reduced(total, x_last):
    return reduce_y(total) if x_last else reduce_x(total)


def plain_gathered(shard):
    own = lax.all_gather(shard, "shard", axis=0, tiled=True)
    arrived = over_section(own)
    is_low = lax.axis_index("section") == 0
    return (jnp.where(is_low, own, arrived), jnp.where(is_low, arrived, own))


def plain_reduced(first, second):
    is_low = lax.axis_index("section") == 0
    kept = jnp.where(is_low, first, second).astype(FLOAT)
    arrived = over_section(jnp.where(is_low, second, first)).astype(FLOAT)
    return lax.psum_scatter(kept + arrived, "shard", scatter_dimension=0, tiled=True)


def forward_attention(hidden, qk, vo, vectors):
    ln1_gain, ln1_bias, out_bias, ln2_gain, ln2_bias, _, qv_bias, _ = [
        item.astype(FLOAT) for item in vectors
    ]
    h_float = hidden.astype(FLOAT)
    normed = norm_affine(h_float, ln1_gain, ln1_bias).astype(LOW)
    key_bias = jnp.concatenate([qv_bias[:D], jnp.zeros((D,), FLOAT)])
    qk_rows = (jnp.dot(normed, qk, preferred_element_type=FLOAT) + key_bias).astype(LOW)
    value_rows = (
        jnp.dot(normed, vo[:, :D], preferred_element_type=FLOAT) + qv_bias[D:]
    ).astype(LOW)
    attended = attention_forward(qk_rows, value_rows)
    residual = h_float + jnp.dot(attended, vo[:, D:], preferred_element_type=FLOAT) + out_bias
    normed_two = norm_affine(residual, ln2_gain, ln2_bias).astype(LOW)
    return (normed, qk_rows, value_rows, attended, residual, normed_two)


def forward_mlp(residual, normed_two, up, down, vectors):
    before = jnp.dot(normed_two, up, preferred_element_type=FLOAT) + vectors[7].astype(FLOAT)
    activated = jax.nn.gelu(before).astype(LOW)
    layer_out = (
        residual
        + jnp.dot(activated, down, preferred_element_type=FLOAT)
        + vectors[5].astype(FLOAT)
    )
    return (before, activated, layer_out)


def backward_mlp(grad_out, before, activated, normed_two, up, down):
    down_bias_grad = jnp.sum(grad_out, axis=0)
    grad_low = grad_out.astype(LOW)
    down_grad = dot_tn(activated, grad_low).astype(LOW)
    grad_act = dot_nt(grad_low, down)
    _, gelu_back = jax.vjp(jax.nn.gelu, before)
    (grad_before,) = gelu_back(grad_act)
    up_bias_grad = jnp.sum(grad_before, axis=0)
    before_low = grad_before.astype(LOW)
    up_grad = dot_tn(normed_two, before_low).astype(LOW)
    grad_normed = dot_nt(before_low, up)
    return (up_grad, down_grad, grad_normed, down_bias_grad, up_bias_grad)


def backward_to_scores(grad_out, grad_normed, residual, attended, qk_rows, value_rows, vo, vectors):
    _, norm_back = jax.vjp(norm_affine, residual, vectors[3].astype(FLOAT), vectors[4].astype(FLOAT))
    grad_norm, gain_grad, bias_grad = norm_back(grad_normed)
    grad_residual = grad_out + grad_norm
    out_bias_grad = jnp.sum(grad_residual, axis=0)
    residual_low = grad_residual.astype(LOW)
    out_grad = dot_tn(attended, residual_low).astype(LOW)
    grad_attended = dot_nt(residual_low, vo[:, D:]).astype(LOW)
    grad_qk, grad_v = attention_backward(qk_rows, value_rows, grad_attended)
    return (grad_residual, out_grad, grad_qk, grad_v, gain_grad, bias_grad, out_bias_grad)


def backward_input(grad_residual, grad_qk, grad_v, hidden, normed, qk, vo, vectors):
    qv_bias_grad = jnp.concatenate(
        [
            jnp.sum(grad_qk[:, :D].astype(FLOAT), axis=0),
            jnp.sum(grad_v.astype(FLOAT), axis=0),
        ]
    )
    qk_grad = dot_tn(normed, grad_qk).astype(LOW)
    v_grad = dot_tn(normed, grad_v).astype(LOW)
    grad_normed = dot_nt(grad_qk, qk) + dot_nt(grad_v, vo[:, :D])
    _, norm_back = jax.vjp(
        norm_affine, hidden.astype(FLOAT), vectors[0].astype(FLOAT), vectors[1].astype(FLOAT)
    )
    grad_norm, gain_grad, bias_grad = norm_back(grad_normed)
    return ((grad_residual + grad_norm).astype(LOW), qk_grad, v_grad, gain_grad, bias_grad, qv_bias_grad)


def on_device(
    boundary,
    ln1_gain,
    ln1_bias,
    w_qkv,
    qv_bias,
    w_out,
    out_bias,
    ln2_gain,
    ln2_bias,
    w_up,
    up_bias,
    w_down,
    down_bias,
):
    x = lax.axis_index("section")
    is_first = x == 0
    count = lax.axis_size("shard")
    direct = count <= 16
    packed = pack_vectors(
        [ln1_gain, ln1_bias, out_bias, ln2_gain, ln2_bias, down_bias], qv_bias, up_bias, 1
    )[0]
    qk_shard = w_qkv[0, :, : 2 * D]
    vo_shard = jnp.concatenate([w_qkv[0, :, 2 * D :], w_out[0]], axis=1)
    traded = jnp.where(is_first, boundary[0, 1], boundary[0, 0])

    if direct:
        qk0, qk1 = halves_of_both(qk_shard)
        vo0, vo1 = halves_of_both(vo_shard)
        up0, up1 = halves_of_both(w_up[0])
        down0, down1 = halves_of_both(w_down[0])
        qk0, qk1, vo0, vo1, up0, up1, down0, down1, packed, traded = tie(
            qk0, qk1, vo0, vo1, up0, up1, down0, down1, packed, traded
        )
        qk0, vo0 = spread_z(qk0), spread_z(vo0)
        other = over_section(traded)
        vectors = gather_vectors(packed)
        qk0, vo0, other, vectors, qk1, vo1, up0, up1, down0, down1 = tie(
            qk0, vo0, other, vectors, qk1, vo1, up0, up1, down0, down1
        )
        qk0, vo0 = second_stage(qk0, True), second_stage(vo0, False)
        qk0, vo0 = third_stage(qk0, True), third_stage(vo0, False)
        up0, down0 = spread_z(up0), spread_z(down0)
        qk0, vo0, up0, down0, qk1, vo1, up1, down1 = tie(
            qk0, vo0, up0, down0, qk1, vo1, up1, down1
        )
        qk0, vo0 = core_stage(qk0), core_stage(vo0)
        up0, down0 = second_stage(up0, True), second_stage(down0, False)
        qk1, vo1 = spread_z(qk1), spread_z(vo1)
        qk0, vo0, up0, down0, qk1, vo1, up1, down1 = tie(
            qk0, vo0, up0, down0, qk1, vo1, up1, down1
        )
    else:
        vectors = gather_vectors(packed)
        other = over_section(traded)
        qk0, qk1 = plain_gathered(qk_shard)
        vo0, vo1 = plain_gathered(vo_shard)
        up0, up1 = plain_gathered(w_up[0])
        down0, down1 = plain_gathered(w_down[0])
    vector0, vector1 = [unpack_vectors(item) for item in vectors]
    hidden = jnp.where(is_first, boundary[0, 0], other)
    cotangent = jnp.where(is_first, other, boundary[0, 1]).astype(FLOAT)

    kept0 = forward_attention(hidden, qk0, vo0, vector0)
    if direct:
        up0, down0 = third_stage(up0, True), third_stage(down0, False)
        up1, down1 = spread_z(up1), spread_z(down1)
        kept0, up0, down0, up1, down1, qk1, vo1 = tie(kept0, up0, down0, up1, down1, qk1, vo1)
        up0, down0 = core_stage(up0), core_stage(down0)
        qk1, vo1 = second_stage(qk1, True), second_stage(vo1, False)
        qk1, vo1 = third_stage(qk1, True), third_stage(vo1, False)
    before0, activated0, out0 = forward_mlp(kept0[4], kept0[5], up0, down0, vector0)
    first_low = out0.astype(LOW)
    if direct:
        first_low, before0, activated0, qk1, vo1, up1, down1 = tie(
            first_low, before0, activated0, qk1, vo1, up1, down1
        )
        qk1, vo1 = core_stage(qk1), core_stage(vo1)
        up1, down1 = second_stage(up1, True), second_stage(down1, False)
        first_low, qk1, vo1, up1, down1 = tie(first_low, qk1, vo1, up1, down1)
    kept1 = forward_attention(first_low, qk1, vo1, vector1)
    if direct:
        up1, down1 = third_stage(up1, True), third_stage(down1, False)
        kept1, up1, down1 = tie(kept1, up1, down1)
        up1, down1 = core_stage(up1), core_stage(down1)
    before1, activated1, out1 = forward_mlp(kept1[4], kept1[5], up1, down1, vector1)
    second_low = out1.astype(LOW)
    sent_out = jnp.where(is_first, second_low, first_low)
    if direct:
        sent_out, before1, activated1, cotangent = tie(sent_out, before1, activated1, cotangent)
    arrived_out = over_section(sent_out)
    mlp1 = backward_mlp(cotangent, before1, activated1, kept1[5], up1, down1)
    if direct:
        mlp1, arrived_out = tie(mlp1, arrived_out)
    up_grad1, down_grad1, grad_normed1, down_bias1, up_bias1 = mlp1
    back1 = backward_to_scores(
        cotangent, grad_normed1, kept1[4], kept1[3], kept1[1], kept1[2], vo1, vector1
    )
    residual1, out_grad1, grad_qk1, grad_v1, ln2_gain1, ln2_bias1, out_bias1 = back1
    mid_low, qk_grad1, v_grad1, ln1_gain1, ln1_bias1, qv_bias1 = backward_input(
        residual1, grad_qk1, grad_v1, first_low, kept1[0], qk1, vo1, vector1
    )
    vo_grad1 = jnp.concatenate([v_grad1, out_grad1], axis=1)
    small1 = pack_vectors(
        [ln1_gain1, ln1_bias1, out_bias1, ln2_gain1, ln2_bias1, down_bias1], qv_bias1, up_bias1, count
    )
    if direct:
        up_sum1, down_sum1 = core_reduced(up_grad1), core_reduced(down_grad1)
        up_sum1, down_sum1 = wide_reduced(up_sum1, True), wide_reduced(down_sum1, False)
        mid_low, qk_grad1, vo_grad1, small1, up_sum1, down_sum1 = tie(
            mid_low, qk_grad1, vo_grad1, small1, up_sum1, down_sum1
        )
        up_sum1, down_sum1 = narrow_reduced(up_sum1, True), narrow_reduced(down_sum1, False)
        qk_sum1, vo_sum1 = core_reduced(qk_grad1), core_reduced(vo_grad1)
    mid_float = mid_low.astype(FLOAT)
    mlp0 = backward_mlp(mid_float, before0, activated0, kept0[5], up0, down0)
    if direct:
        mlp0, up_sum1, down_sum1, qk_sum1, vo_sum1, mid_float = tie(
            mlp0, up_sum1, down_sum1, qk_sum1, vo_sum1, mid_float
        )
    up_grad0, down_grad0, grad_normed0, down_bias0, up_bias0 = mlp0
    back0 = backward_to_scores(
        mid_float, grad_normed0, kept0[4], kept0[3], kept0[1], kept0[2], vo0, vector0
    )
    if direct:
        up_sum0, down_sum0 = core_reduced(up_grad0), core_reduced(down_grad0)
        qk_sum1, vo_sum1 = wide_reduced(qk_sum1, True), wide_reduced(vo_sum1, False)
        up_sum1, down_sum1 = reduce_z(up_sum1), reduce_z(down_sum1)
        back0, up_sum0, down_sum0, qk_sum1, vo_sum1, up_sum1, down_sum1 = tie(
            back0, up_sum0, down_sum0, qk_sum1, vo_sum1, up_sum1, down_sum1
        )
    residual0, out_grad0, grad_qk0, grad_v0, ln2_gain0, ln2_bias0, out_bias0 = back0
    in_low, qk_grad0, v_grad0, ln1_gain0, ln1_bias0, qv_bias0 = backward_input(
        residual0, grad_qk0, grad_v0, hidden, kept0[0], qk0, vo0, vector0
    )
    vo_grad0 = jnp.concatenate([v_grad0, out_grad0], axis=1)
    small0 = pack_vectors(
        [ln1_gain0, ln1_bias0, out_bias0, ln2_gain0, ln2_bias0, down_bias0], qv_bias0, up_bias0, count
    )
    sent_grad = jnp.where(is_first, mid_low, in_low)
    if direct:
        up_sum0, down_sum0 = wide_reduced(up_sum0, True), wide_reduced(down_sum0, False)
        qk_grad0, vo_grad0, small0, sent_grad, up_sum0, down_sum0, qk_sum1, vo_sum1 = tie(
            qk_grad0, vo_grad0, small0, sent_grad, up_sum0, down_sum0, qk_sum1, vo_sum1
        )
        qk_sum0, vo_sum0 = core_reduced(qk_grad0), core_reduced(vo_grad0)
        qk_sum1, vo_sum1 = narrow_reduced(qk_sum1, True), narrow_reduced(vo_sum1, False)
        up_sum0, down_sum0 = narrow_reduced(up_sum0, True), narrow_reduced(down_sum0, False)
        qk_sum0, vo_sum0, qk_sum1, vo_sum1, up_sum0, down_sum0, small0, small1, sent_grad = tie(
            qk_sum0, vo_sum0, qk_sum1, vo_sum1, up_sum0, down_sum0, small0, small1, sent_grad
        )
        up_sum0, down_sum0 = reduce_z(up_sum0), reduce_z(down_sum0)
        qk_sum1, vo_sum1 = reduce_z(qk_sum1), reduce_z(vo_sum1)
        qk_sum0, vo_sum0 = wide_reduced(qk_sum0, True), wide_reduced(vo_sum0, False)
        qk_sum0, vo_sum0 = narrow_reduced(qk_sum0, True), narrow_reduced(vo_sum0, False)
        vector = scatter_vectors(small0, small1)
        qk_sum0, vo_sum0, qk_sum1, vo_sum1, up_sum0, down_sum0, sent_grad, vector = tie(
            qk_sum0, vo_sum0, qk_sum1, vo_sum1, up_sum0, down_sum0, sent_grad, vector
        )
        arrived_grad = over_section(sent_grad)
        up, down = join_halves(up_sum0, up_sum1), join_halves(down_sum0, down_sum1)
        qk_sum0, vo_sum0 = reduce_z(qk_sum0), reduce_z(vo_sum0)
        qk, vo = join_halves(qk_sum0, qk_sum1), join_halves(vo_sum0, vo_sum1)
    else:
        arrived_grad = over_section(sent_grad)
        vector = scatter_vectors(small0, small1)
        qk, vo = plain_reduced(qk_grad0, qk_grad1), plain_reduced(vo_grad0, vo_grad1)
        up, down = plain_reduced(up_grad0, up_grad1), plain_reduced(down_grad0, down_grad1)
    own_out = jnp.where(is_first, first_low, second_low)
    own_grad = jnp.where(is_first, in_low, mid_low)
    section_outputs = jnp.where(
        is_first, jnp.stack([own_out, arrived_out]), jnp.stack([arrived_out, own_out])
    )[None]
    section_grads = jnp.where(
        is_first, jnp.stack([own_grad, arrived_grad]), jnp.stack([arrived_grad, own_grad])
    )[None]
    return (
        section_outputs,
        section_grads,
        vector[0:1],
        vector[1:2],
        jnp.concatenate([qk, vo[:, :D]], axis=1)[None],
        vector[6:8].reshape(1, -1),
        vo[:, D:][None],
        vector[2:3],
        vector[3:4],
        vector[4:5],
        up[None],
        vector[8:12].reshape(1, -1),
        down[None],
        vector[5:6],
    )


def solution(mesh):
    placed = (
        P("section", None, "shard", None),
        P("section", "shard"),
        P("section", "shard"),
        P("section", "shard", None),
        P("section", "shard"),
        P("section", "shard", None),
        P("section", "shard"),
        P("section", "shard"),
        P("section", "shard"),
        P("section", "shard", None),
        P("section", "shard"),
        P("section", "shard", None),
        P("section", "shard"),
    )
    return jax.shard_map(
        on_device,
        mesh=mesh,
        in_specs=placed,
        out_specs=(
            P("section", None, "shard", None),
            P("section", None, "shard", None),
            P("section", "shard"),
            P("section", "shard"),
            P("section", "shard", None),
            P("section", "shard"),
            P("section", "shard", None),
            P("section", "shard"),
            P("section", "shard"),
            P("section", "shard"),
            P("section", "shard", None),
            P("section", "shard"),
            P("section", "shard", None),
            P("section", "shard"),
        ),
        check_vma=False,
    )
```

```python
import jax
import jax.numpy as jnp
from jax import lax
from jax.experimental import pallas as pl
from jax.experimental.pallas import tpu as pltpu
from jax.sharding import PartitionSpec as P

D = 768
LOW = jnp.bfloat16
FLOAT = jnp.float32
CHUNK = 256


def norm_affine(values, gain, bias):
    row_mean = jnp.mean(values, axis=-1, keepdims=True)
    centred = values - row_mean
    variance = jnp.mean(centred * centred, axis=-1, keepdims=True)
    return centred * lax.rsqrt(variance + 1e-05) * gain + bias


def dot_nt(a,b):
    return lax.dot_general(a,b,(((1,),(1,)),((),())),preferred_element_type=FLOAT)


def dot_nn(a,b):
    return lax.dot_general(a,b,(((1,),(0,)),((),())),preferred_element_type=FLOAT)


def dot_tn(a,b):
    return lax.dot_general(a,b,(((0,),(0,)),((),())),preferred_element_type=FLOAT)


def head_part(block, head):
    lane = lax.broadcasted_iota(jnp.int32, block.shape, 1)
    return jnp.where((lane >= 64) == (head == 1), block, jnp.zeros_like(block))


def probabilities(q_rows, k_rows, first):
    scores = dot_nt(q_rows, k_rows)
    row = lax.broadcasted_iota(jnp.int32, scores.shape, 0) + first
    col = lax.broadcasted_iota(jnp.int32, scores.shape, 1)
    scores = jnp.where(col <= row, scores, -1e30)
    top = jnp.max(scores, axis=-1, keepdims=True)
    exponent = jnp.exp(scores - top)
    return exponent * (1.0 / jnp.sum(exponent, axis=-1, keepdims=True))


def fwd_kernel(q_ref, k_ref, v_ref, o_ref):
    rows = q_ref.shape[0]
    k = k_ref[...]; v = v_ref[...]
    for first in range(0, rows, CHUNK):
        last = first + CHUNK
        q = q_ref[first:last, :] * LOW(0.125)
        total = None
        for head in range(2):
            p = probabilities(head_part(q, head), k[:last], first).astype(LOW)
            part = dot_nn(p, head_part(v[:last], head))
            total = part if total is None else total + part
        o_ref[first:last, :] = total.astype(LOW)


def attention_forward(qk, values):
    rows = qk.shape[0]
    pairs = D // 128
    first = pl.BlockSpec((rows, 128), lambda pair: (0, pair))
    second = pl.BlockSpec((rows, 128), lambda pair: (0, pair + pairs))
    return pl.pallas_call(
        fwd_kernel,
        grid=(pairs,),
        in_specs=[first, second, first],
        out_specs=first,
        out_shape=jax.ShapeDtypeStruct((rows, D), LOW),
        compiler_params=pltpu.CompilerParams(vmem_limit_bytes=32 * 1024 * 1024),
        cost_estimate=pl.CostEstimate(
            flops=rows * rows * D, bytes_accessed=8 * rows * D, transcendentals=0
        ),
        name="attend_forward",
    )(qk, qk, values)


def bwd_kernel(q_ref, k_ref, v_ref, g_ref, qk_out, v_out, dk_acc, dv_acc):
    rows = q_ref.shape[0]
    h = pl.program_id(0)
    k = k_ref[...]; v = v_ref[...]
    dk_acc[...] = jnp.zeros_like(dk_acc)
    dv_acc[...] = jnp.zeros_like(dv_acc)
    col = pl.multiple_of(h * 128, 128)
    for first in range(0, rows, CHUNK):
        last = first + CHUNK
        q = q_ref[first:last, :] * LOW(0.125)
        g = g_ref[first:last, :]
        dq = None
        for head in range(2):
            qh = head_part(q, head); gh = head_part(g, head)
            p = probabilities(qh, k[:last], first)
            dp = dot_nt(gh, v[:last])
            centre = jnp.sum(p * dp, axis=-1, keepdims=True)
            ds = (p * (dp - centre)).astype(LOW)
            part = dot_nn(ds, head_part(k[:last], head))
            dq = part if dq is None else dq + part
            dk_acc[:last, :] += dot_tn(ds, qh)
            dv_acc[:last, :] += dot_tn(p.astype(LOW), gh)
        qk_out[first:last, pl.ds(col, 128)] = (dq * 0.125).astype(LOW)
    qk_out[:, pl.ds(D + col, 128)] = dk_acc[...].astype(LOW)
    v_out[...] = dv_acc[...].astype(LOW)


def attention_backward(qk, values, grad):
    rows = qk.shape[0]
    pairs = D // 128
    first = pl.BlockSpec((rows, 128), lambda pair: (0, pair))
    second = pl.BlockSpec((rows, 128), lambda pair: (0, pair + pairs))
    return pl.pallas_call(
        bwd_kernel,
        grid=(pairs,),
        in_specs=[first, second, first, first],
        out_specs=[pl.BlockSpec((rows, 2 * D), lambda pair: (0, 0)), first],
        out_shape=[
            jax.ShapeDtypeStruct((rows, 2 * D), LOW),
            jax.ShapeDtypeStruct((rows, D), LOW),
        ],
        scratch_shapes=[pltpu.VMEM((rows, 128), FLOAT), pltpu.VMEM((rows, 128), FLOAT)],
        compiler_params=pltpu.CompilerParams(vmem_limit_bytes=32 * 1024 * 1024),
        cost_estimate=pl.CostEstimate(
            flops=rows * rows * D, bytes_accessed=14 * rows * D, transcendentals=0
        ),
        name="attend_backward",
    )(qk, qk, values, grad)


def hop(value, axis, target):
    count = lax.axis_size(axis)
    return lax.ppermute(value, axis, [(source, target(source)) for source in range(count)])


def over_section(value):
    return hop(value, "section", lambda source: 1 - source)


def over_core(value):
    return hop(value, "shard", lambda source: source ^ 1)


def over_y(value):
    return hop(value, "shard", lambda source: source ^ 2)


def over_z(value, steps):
    count = lax.axis_size("shard")
    return hop(value, "shard", lambda source: (source + 4 * steps) % count)


def place(buffer, block, index, dim):
    starts = [0] * buffer.ndim
    starts[dim] = index
    return lax.dynamic_update_slice(buffer, block, starts)


def take(value, index, size, dim):
    return lax.dynamic_slice_in_dim(value, index * size, size, dim)


def place_of():
    shard = lax.axis_index("shard")
    return (lax.axis_index("section"), shard // 4, (shard // 2) % 2, shard % 2)


def spread_z(block):
    _, z, _, _ = place_of()
    count = lax.axis_size("shard") // 4
    buffer = jnp.zeros((count,) + block.shape, block.dtype)
    buffer = place(buffer, block[None], z, 0)
    for steps in range(1, count):
        arrived = over_z(block, steps)
        buffer = place(buffer, arrived[None], (z - steps) % count, 0)
    return buffer


def pair(own, arrived, index, dim):
    own, arrived = jnp.expand_dims(own, dim), jnp.expand_dims(arrived, dim)
    is_low = index == 0
    return jnp.concatenate(
        [jnp.where(is_low, own, arrived), jnp.where(is_low, arrived, own)], axis=dim
    )


def spread_y(blocks):
    _, _, y, _ = place_of()
    return pair(blocks, over_y(blocks), y, 1)


def spread_x(blocks):
    x, _, _, _ = place_of()
    return pair(blocks, over_section(blocks), x, blocks.ndim - 2)


def spread_core(blocks):
    _, _, _, core = place_of()
    return pair(blocks, over_core(blocks), core, 2)


def halves_of_both(shard):
    x, _, _, _ = place_of()
    half = shard.shape[0] // 2
    own = take(shard, x, half, 0)
    arrived = over_section(take(shard, 1 - x, half, 0))
    is_low = x == 0
    return (jnp.where(is_low, own, arrived), jnp.where(is_low, arrived, own))


def gather_vectors(packed):
    x, _, y, core = place_of()
    stacked = spread_z(packed)
    stacked = pair(stacked, over_y(stacked), y, 1)
    stacked = pair(stacked, over_core(stacked), core, 2)
    stacked = stacked.reshape((-1,) + packed.shape)
    arrived = over_section(stacked)
    return (jnp.where(x == 0, stacked, arrived), jnp.where(x == 0, arrived, stacked))


def reduce_pair(total, index, dim, exchange):
    sent = lax.dynamic_index_in_dim(total, 1 - index, dim, keepdims=False)
    kept = lax.dynamic_index_in_dim(total, index, dim, keepdims=False)
    return (kept.astype(FLOAT) + exchange(sent).astype(FLOAT)).astype(LOW)


def reduce_core(total):
    return reduce_pair(total, place_of()[3], 2, over_core)


def reduce_y(total):
    return reduce_pair(total, place_of()[2], 1, over_y)


def reduce_x(total):
    return reduce_pair(total, place_of()[0], total.ndim - 3, over_section)


def reduce_z(total):
    _, z, _, _ = place_of()
    count = total.shape[0]
    result = lax.dynamic_index_in_dim(total, z, 0, keepdims=False).astype(FLOAT)
    for steps in range(1, count):
        sent = lax.dynamic_index_in_dim(total, (z + steps) % count, 0, keepdims=False)
        result = result + over_z(sent, steps).astype(FLOAT)
    return result


def join_halves(first_layer, second_layer):
    x, _, _, _ = place_of()
    is_low = x == 0
    kept = jnp.where(is_low, first_layer, second_layer)
    arrived = over_section(jnp.where(is_low, second_layer, first_layer).astype(LOW)).astype(FLOAT)
    return jnp.concatenate(
        [jnp.where(is_low, kept, arrived), jnp.where(is_low, arrived, kept)], axis=0
    )


def scatter_vectors(first_layer, second_layer):
    x, z, y, core = place_of()
    count = lax.axis_size("shard")
    is_low = x == 0
    kept = jnp.where(is_low, first_layer, second_layer)
    total = kept + over_section(jnp.where(is_low, second_layer, first_layer))
    total = total.reshape((count // 4, 2, 2) + total.shape[1:])
    sent = lax.dynamic_index_in_dim(total, 1 - core, 2, keepdims=False)
    total = lax.dynamic_index_in_dim(total, core, 2, keepdims=False) + over_core(sent)
    sent = lax.dynamic_index_in_dim(total, 1 - y, 1, keepdims=False)
    total = lax.dynamic_index_in_dim(total, y, 1, keepdims=False) + over_y(sent)
    return reduce_z(total)


def unpack_vectors(stacked):
    rows = stacked.shape[0]
    singles = [stacked[:, item].reshape(-1) for item in range(6)]
    return singles + [stacked[:, 6:8].reshape(-1), stacked[:, 8:12].reshape(-1)]


def pack_vectors(singles, pair_vector, quad_vector, count):
    parts = [item.reshape(count, 1, -1) for item in singles]
    parts.append(pair_vector.reshape(count, 2, -1))
    parts.append(quad_vector.reshape(count, 4, -1))
    return jnp.concatenate(parts, axis=1)


def plain_gathered(shard):
    own = lax.all_gather(shard, "shard", axis=0, tiled=True)
    arrived = over_section(own)
    is_low = lax.axis_index("section") == 0
    return (jnp.where(is_low, own, arrived), jnp.where(is_low, arrived, own))


def plain_reduced(first, second):
    is_low = lax.axis_index("section") == 0
    kept = jnp.where(is_low, first, second).astype(FLOAT)
    arrived = over_section(jnp.where(is_low, second, first)).astype(FLOAT)
    return lax.psum_scatter(kept + arrived, "shard", scatter_dimension=0, tiled=True)


def forward_attention(hidden, qk, vo, vectors):
    ln1_gain, ln1_bias, out_bias, ln2_gain, ln2_bias, _, qv_bias, _ = [
        item.astype(FLOAT) for item in vectors
    ]
    h_float = hidden.astype(FLOAT)
    normed = norm_affine(h_float, ln1_gain, ln1_bias).astype(LOW)
    key_bias = jnp.concatenate([qv_bias[:D], jnp.zeros((D,), FLOAT)])
    qk_rows = (jnp.dot(normed, qk, preferred_element_type=FLOAT) + key_bias).astype(LOW)
    value_rows = (
        jnp.dot(normed, vo[:, :D], preferred_element_type=FLOAT) + qv_bias[D:]
    ).astype(LOW)
    attended = attention_forward(qk_rows, value_rows)
    residual = h_float + jnp.dot(attended, vo[:, D:], preferred_element_type=FLOAT) + out_bias
    normed_two = norm_affine(residual, ln2_gain, ln2_bias).astype(LOW)
    return (normed, qk_rows, value_rows, attended, residual, normed_two)


def forward_mlp(residual, normed_two, up, down, vectors):
    before = jnp.dot(normed_two, up, preferred_element_type=FLOAT) + vectors[7].astype(FLOAT)
    activated = jax.nn.gelu(before).astype(LOW)
    layer_out = (
        residual
        + jnp.dot(activated, down, preferred_element_type=FLOAT)
        + vectors[5].astype(FLOAT)
    )
    return (before, activated, layer_out)


def backward_mlp(grad_out, before, activated, normed_two, up, down):
    down_bias_grad = jnp.sum(grad_out, axis=0)
    grad_low = grad_out.astype(LOW)
    down_grad = dot_tn(activated, grad_low).astype(LOW)
    grad_act = dot_nt(grad_low, down)
    _, gelu_back = jax.vjp(jax.nn.gelu, before)
    (grad_before,) = gelu_back(grad_act)
    up_bias_grad = jnp.sum(grad_before, axis=0)
    before_low = grad_before.astype(LOW)
    up_grad = dot_tn(normed_two, before_low).astype(LOW)
    grad_normed = dot_nt(before_low, up)
    return (up_grad, down_grad, grad_normed, down_bias_grad, up_bias_grad)


def backward_to_scores(grad_out, grad_normed, residual, attended, qk_rows, value_rows, vo, vectors):
    _, norm_back = jax.vjp(norm_affine, residual, vectors[3].astype(FLOAT), vectors[4].astype(FLOAT))
    grad_norm, gain_grad, bias_grad = norm_back(grad_normed)
    grad_residual = grad_out + grad_norm
    out_bias_grad = jnp.sum(grad_residual, axis=0)
    residual_low = grad_residual.astype(LOW)
    out_grad = dot_tn(attended, residual_low).astype(LOW)
    grad_attended = dot_nt(residual_low, vo[:, D:]).astype(LOW)
    grad_qk, grad_v = attention_backward(qk_rows, value_rows, grad_attended)
    return (grad_residual, out_grad, grad_qk, grad_v, gain_grad, bias_grad, out_bias_grad)


def backward_input(grad_residual, grad_qk, grad_v, hidden, qk, vo, vectors):
    qv_bias_grad = jnp.concatenate(
        [
            jnp.sum(grad_qk[:, :D].astype(FLOAT), axis=0),
            jnp.sum(grad_v.astype(FLOAT), axis=0),
        ]
    )
    grad_normed = dot_nt(grad_qk, qk) + dot_nt(grad_v, vo[:, :D])
    _, norm_back = jax.vjp(
        norm_affine, hidden.astype(FLOAT), vectors[0].astype(FLOAT), vectors[1].astype(FLOAT)
    )
    grad_norm, gain_grad, bias_grad = norm_back(grad_normed)
    return ((grad_residual + grad_norm).astype(LOW), gain_grad, bias_grad, qv_bias_grad)


def tie(*values):
    return lax.optimization_barrier(values)


def second_stage(stacked, x_last):
    return spread_y(stacked) if x_last else spread_x(stacked)


def third_stage(stacked, x_last):
    return spread_x(stacked) if x_last else spread_y(stacked)


def core_stage(stacked):
    stacked = spread_core(stacked)
    return stacked.reshape(-1, stacked.shape[-1])


def core_reduced(total):
    count = lax.axis_size("shard")
    return reduce_core(
        total.reshape(count // 4, 2, 2, 2, total.shape[0] // (2 * count), total.shape[1])
    )


def wide_reduced(total, x_last):
    return reduce_x(total) if x_last else reduce_y(total)


def narrow_reduced(total, x_last):
    return reduce_y(total) if x_last else reduce_x(total)


def whole_gathered(main, down):
    columns = main.shape[1] // 4
    groups = [main[:, columns * item : columns * (item + 1)] for item in range(4)]
    packed = jnp.concatenate([jnp.concatenate(groups, axis=0), down], axis=1)
    return lax.all_gather(packed, ("shard", "section"), axis=0, tiled=True)


def parts_of(whole, devices):
    columns = whole.shape[1] - D
    main = whole[:, :columns].reshape(devices, 4, -1, columns)
    qk, vo, up_low, up_high = [main[:, item].reshape(-1, columns) for item in range(4)]
    return (qk, vo, jnp.concatenate([up_low, up_high], axis=1), whole[:, columns:])


def mlp_packed(up_grad, down_grad):
    count = lax.axis_size("shard")
    rows = D // (2 * count)
    blocks = down_grad.reshape(2 * count, -1, rows, D).transpose(0, 2, 1, 3)
    return jnp.concatenate([up_grad, blocks.reshape(D, -1)], axis=1)


def mlp_scattered(total, columns):
    rows = D // (2 * lax.axis_size("shard"))
    total = lax.psum_scatter(total, ("shard", "section"), scatter_dimension=0, tiled=True)
    total = total.astype(FLOAT)
    down = total[:, columns:].reshape(rows, -1, D).transpose(1, 0, 2).reshape(-1, D)
    return (total[:, :columns], down)


def on_device(
    boundary,
    ln1_gain,
    ln1_bias,
    w_qkv,
    qv_bias,
    w_out,
    out_bias,
    ln2_gain,
    ln2_bias,
    w_up,
    up_bias,
    w_down,
    down_bias,
):
    x = lax.axis_index("section")
    is_first = x == 0
    count = lax.axis_size("shard")
    direct = count <= 16
    cut = 4 * D
    packed = pack_vectors(
        [ln1_gain, ln1_bias, out_bias, ln2_gain, ln2_bias, down_bias], qv_bias, up_bias, 1
    )[0]
    main_shard = jnp.concatenate([w_qkv[0], w_out[0], w_up[0]], axis=1)
    traded = jnp.where(is_first, boundary[0, 1], boundary[0, 0])

    if direct:
        main0, main1 = halves_of_both(main_shard)
        down0, down1 = halves_of_both(w_down[0])
        main0, main1, down0, down1, packed, traded = tie(
            main0, main1, down0, down1, packed, traded
        )
        whole1 = whole_gathered(main1, down1)
        first_part, up0 = main0[:, :cut], main0[:, cut:]
        first_part = spread_z(first_part)
        vectors = gather_vectors(packed)
        first_part, up0, down0, traded = tie(first_part, up0, down0, traded)
        other = over_section(traded)
        qk0 = third_stage(second_stage(first_part[..., : 2 * D], True), True)
        vo0 = third_stage(second_stage(first_part[..., 2 * D :], False), False)
        up0, down0 = spread_z(up0), spread_z(down0)
        qk0, vo0, up0, down0 = tie(qk0, vo0, up0, down0)
        qk0, vo0 = core_stage(qk0), core_stage(vo0)
        up0, down0 = second_stage(up0, True), second_stage(down0, False)
        qk0, vo0, up0, down0 = tie(qk0, vo0, up0, down0)
    else:
        vectors = gather_vectors(packed)
        other = over_section(traded)
        main0, main1 = plain_gathered(main_shard)
        down0, down1 = plain_gathered(w_down[0])
        qk0, vo0, up0 = main0[:, : 2 * D], main0[:, 2 * D : cut], main0[:, cut:]
    vector0, vector1 = [unpack_vectors(item) for item in vectors]
    hidden = jnp.where(is_first, boundary[0, 0], other)
    cotangent = jnp.where(is_first, other, boundary[0, 1]).astype(FLOAT)

    kept0 = forward_attention(hidden, qk0, vo0, vector0)
    if direct:
        up0, down0 = third_stage(up0, True), third_stage(down0, False)
        kept0, up0, down0 = tie(kept0, up0, down0)
        up0, down0 = core_stage(up0), core_stage(down0)
    before0, activated0, out0 = forward_mlp(kept0[4], kept0[5], up0, down0, vector0)
    first_low = out0.astype(LOW)
    if direct:
        first_low, whole1 = tie(first_low, whole1)
        qk1, vo1, up1, down1 = parts_of(whole1, 2 * count)
    else:
        qk1, vo1, up1 = main1[:, : 2 * D], main1[:, 2 * D : cut], main1[:, cut:]
    kept1 = forward_attention(first_low, qk1, vo1, vector1)
    before1, activated1, out1 = forward_mlp(kept1[4], kept1[5], up1, down1, vector1)
    second_low = out1.astype(LOW)
    sent_out = jnp.where(is_first, second_low, first_low)
    if direct:
        sent_out, before1, activated1, cotangent = tie(sent_out, before1, activated1, cotangent)
    arrived_out = over_section(sent_out)
    mlp1 = backward_mlp(cotangent, before1, activated1, kept1[5], up1, down1)
    if direct:
        total1 = mlp_packed(mlp1[0], mlp1[1])
        mlp1, arrived_out, total1 = tie(mlp1, arrived_out, total1)
    up_grad1, down_grad1, grad_normed1, down_bias1, up_bias1 = mlp1
    back1 = backward_to_scores(
        cotangent, grad_normed1, kept1[4], kept1[3], kept1[1], kept1[2], vo1, vector1
    )
    residual1, out_grad1, grad_qk1, grad_v1, ln2_gain1, ln2_bias1, out_bias1 = back1
    mid_low, ln1_gain1, ln1_bias1, qv_bias1 = backward_input(
        residual1, grad_qk1, grad_v1, first_low, qk1, vo1, vector1
    )
    part_grad1 = jnp.concatenate(
        [
            dot_tn(kept1[0], grad_qk1).astype(LOW),
            dot_tn(kept1[0], grad_v1).astype(LOW),
            out_grad1,
        ],
        axis=1,
    )
    small1 = pack_vectors(
        [ln1_gain1, ln1_bias1, out_bias1, ln2_gain1, ln2_bias1, down_bias1], qv_bias1, up_bias1, count
    )
    if direct:
        up_sum1, down_sum1 = mlp_scattered(total1, 4 * D)
        mid_low, part_grad1, small1 = tie(mid_low, part_grad1, small1)
        part_sum1 = core_reduced(part_grad1)
        qk_sum1 = wide_reduced(part_sum1[..., : 2 * D], True)
        vo_sum1 = wide_reduced(part_sum1[..., 2 * D :], False)
    mid_float = mid_low.astype(FLOAT)
    mlp0 = backward_mlp(mid_float, before0, activated0, kept0[5], up0, down0)
    if direct:
        mlp0, qk_sum1, vo_sum1, mid_float = tie(mlp0, qk_sum1, vo_sum1, mid_float)
    up_grad0, down_grad0, grad_normed0, down_bias0, up_bias0 = mlp0
    back0 = backward_to_scores(
        mid_float, grad_normed0, kept0[4], kept0[3], kept0[1], kept0[2], vo0, vector0
    )
    if direct:
        up_sum0, down_sum0 = core_reduced(up_grad0), core_reduced(down_grad0)
        part_sum1 = jnp.concatenate(
            [narrow_reduced(qk_sum1, True), narrow_reduced(vo_sum1, False)], axis=-1
        )
        up_sum0, down_sum0 = wide_reduced(up_sum0, True), wide_reduced(down_sum0, False)
        back0, part_sum1 = tie(back0, part_sum1)
    residual0, out_grad0, grad_qk0, grad_v0, ln2_gain0, ln2_bias0, out_bias0 = back0
    part_grad0 = jnp.concatenate(
        [
            dot_tn(kept0[0], grad_qk0).astype(LOW),
            dot_tn(kept0[0], grad_v0).astype(LOW),
            out_grad0,
        ],
        axis=1,
    )
    if direct:
        part_grad0, up_sum1, down_sum1, part_sum1, residual0, grad_qk0, grad_v0 = tie(
            part_grad0, up_sum1, down_sum1, part_sum1, residual0, grad_qk0, grad_v0
        )
        part_sum0 = core_reduced(part_grad0)
        up_sum0, down_sum0 = narrow_reduced(up_sum0, True), narrow_reduced(down_sum0, False)
    in_low, ln1_gain0, ln1_bias0, qv_bias0 = backward_input(
        residual0, grad_qk0, grad_v0, hidden, qk0, vo0, vector0
    )
    small0 = pack_vectors(
        [ln1_gain0, ln1_bias0, out_bias0, ln2_gain0, ln2_bias0, down_bias0], qv_bias0, up_bias0, count
    )
    sent_grad = jnp.where(is_first, mid_low, in_low)
    if direct:
        part_sum1 = reduce_z(part_sum1)
        qk_sum0 = wide_reduced(part_sum0[..., : 2 * D], True)
        vo_sum0 = wide_reduced(part_sum0[..., 2 * D :], False)
        up_sum0, down_sum0 = reduce_z(up_sum0), reduce_z(down_sum0)
        part_sum0 = jnp.concatenate(
            [narrow_reduced(qk_sum0, True), narrow_reduced(vo_sum0, False)], axis=-1
        )
        vector = scatter_vectors(small0, small1)
        arrived_grad = over_section(sent_grad)
        up, down = join_halves(up_sum0, up_sum1), join_halves(down_sum0, down_sum1)
        part = join_halves(reduce_z(part_sum0), part_sum1)
    else:
        arrived_grad = over_section(sent_grad)
        vector = scatter_vectors(small0, small1)
        part = plain_reduced(part_grad0, part_grad1)
        up, down = plain_reduced(up_grad0, up_grad1), plain_reduced(down_grad0, down_grad1)
    own_out = jnp.where(is_first, first_low, second_low)
    own_grad = jnp.where(is_first, in_low, mid_low)
    section_outputs = jnp.where(
        is_first, jnp.stack([own_out, arrived_out]), jnp.stack([arrived_out, own_out])
    )[None]
    section_grads = jnp.where(
        is_first, jnp.stack([own_grad, arrived_grad]), jnp.stack([arrived_grad, own_grad])
    )[None]
    return (
        section_outputs,
        section_grads,
        vector[0:1],
        vector[1:2],
        part[:, : 3 * D][None],
        vector[6:8].reshape(1, -1),
        part[:, 3 * D :][None],
        vector[2:3],
        vector[3:4],
        vector[4:5],
        up[None],
        vector[8:12].reshape(1, -1),
        down[None],
        vector[5:6],
    )


def solution(mesh):
    placed = (
        P("section", None, "shard", None),
        P("section", "shard"),
        P("section", "shard"),
        P("section", "shard", None),
        P("section", "shard"),
        P("section", "shard", None),
        P("section", "shard"),
        P("section", "shard"),
        P("section", "shard"),
        P("section", "shard", None),
        P("section", "shard"),
        P("section", "shard", None),
        P("section", "shard"),
    )
    return jax.shard_map(
        on_device,
        mesh=mesh,
        in_specs=placed,
        out_specs=(
            P("section", None, "shard", None),
            P("section", None, "shard", None),
            P("section", "shard"),
            P("section", "shard"),
            P("section", "shard", None),
            P("section", "shard"),
            P("section", "shard", None),
            P("section", "shard"),
            P("section", "shard"),
            P("section", "shard"),
            P("section", "shard", None),
            P("section", "shard"),
            P("section", "shard", None),
            P("section", "shard"),
        ),
        check_vma=False,
    )
```

```python
import jax
import jax.numpy as jnp
from jax import lax
from jax.experimental import pallas as pl
from jax.experimental.pallas import tpu as pltpu
from jax.sharding import PartitionSpec as P

D = 768
LOW = jnp.bfloat16
FLOAT = jnp.float32
CHUNK = 256


def norm_affine(values, gain, bias):
    row_mean = jnp.mean(values, axis=-1, keepdims=True)
    centred = values - row_mean
    variance = jnp.mean(centred * centred, axis=-1, keepdims=True)
    return centred * lax.rsqrt(variance + 1e-05) * gain + bias


def dot_nt(a,b):
    return lax.dot_general(a,b,(((1,),(1,)),((),())),preferred_element_type=FLOAT)


def dot_nn(a,b):
    return lax.dot_general(a,b,(((1,),(0,)),((),())),preferred_element_type=FLOAT)


def dot_tn(a,b):
    return lax.dot_general(a,b,(((0,),(0,)),((),())),preferred_element_type=FLOAT)


def head_part(block, head):
    lane = lax.broadcasted_iota(jnp.int32, block.shape, 1)
    return jnp.where((lane >= 64) == (head == 1), block, jnp.zeros_like(block))


def probabilities(q_rows, k_rows, first):
    scores = dot_nt(q_rows, k_rows)
    row = lax.broadcasted_iota(jnp.int32, scores.shape, 0) + first
    col = lax.broadcasted_iota(jnp.int32, scores.shape, 1)
    scores = jnp.where(col <= row, scores, -1e30)
    top = jnp.max(scores, axis=-1, keepdims=True)
    exponent = jnp.exp(scores - top)
    return exponent * (1.0 / jnp.sum(exponent, axis=-1, keepdims=True))


def fwd_kernel(q_ref, k_ref, v_ref, o_ref):
    rows = q_ref.shape[0]
    k = k_ref[...]; v = v_ref[...]
    for first in range(0, rows, CHUNK):
        last = first + CHUNK
        q = q_ref[first:last, :] * LOW(0.125)
        total = None
        for head in range(2):
            p = probabilities(head_part(q, head), k[:last], first).astype(LOW)
            part = dot_nn(p, head_part(v[:last], head))
            total = part if total is None else total + part
        o_ref[first:last, :] = total.astype(LOW)


def attention_forward(qk, values):
    rows = qk.shape[0]
    pairs = D // 128
    first = pl.BlockSpec((rows, 128), lambda pair: (0, pair))
    second = pl.BlockSpec((rows, 128), lambda pair: (0, pair + pairs))
    return pl.pallas_call(
        fwd_kernel,
        grid=(pairs,),
        in_specs=[first, second, first],
        out_specs=first,
        out_shape=jax.ShapeDtypeStruct((rows, D), LOW),
        compiler_params=pltpu.CompilerParams(vmem_limit_bytes=32 * 1024 * 1024),
        cost_estimate=pl.CostEstimate(
            flops=rows * rows * D, bytes_accessed=8 * rows * D, transcendentals=0
        ),
        name="attend_forward",
    )(qk, qk, values)


def bwd_kernel(q_ref, k_ref, v_ref, g_ref, qk_out, v_out, dk_acc, dv_acc):
    rows = q_ref.shape[0]
    h = pl.program_id(0)
    k = k_ref[...]; v = v_ref[...]
    dk_acc[...] = jnp.zeros_like(dk_acc)
    dv_acc[...] = jnp.zeros_like(dv_acc)
    col = pl.multiple_of(h * 128, 128)
    for first in range(0, rows, CHUNK):
        last = first + CHUNK
        q = q_ref[first:last, :] * LOW(0.125)
        g = g_ref[first:last, :]
        dq = None
        for head in range(2):
            qh = head_part(q, head); gh = head_part(g, head)
            p = probabilities(qh, k[:last], first)
            dp = dot_nt(gh, v[:last])
            centre = jnp.sum(p * dp, axis=-1, keepdims=True)
            ds = (p * (dp - centre)).astype(LOW)
            part = dot_nn(ds, head_part(k[:last], head))
            dq = part if dq is None else dq + part
            dk_acc[:last, :] += dot_tn(ds, qh)
            dv_acc[:last, :] += dot_tn(p.astype(LOW), gh)
        qk_out[first:last, pl.ds(col, 128)] = (dq * 0.125).astype(LOW)
    qk_out[:, pl.ds(D + col, 128)] = dk_acc[...].astype(LOW)
    v_out[...] = dv_acc[...].astype(LOW)


def attention_backward(qk, values, grad):
    rows = qk.shape[0]
    pairs = D // 128
    first = pl.BlockSpec((rows, 128), lambda pair: (0, pair))
    second = pl.BlockSpec((rows, 128), lambda pair: (0, pair + pairs))
    return pl.pallas_call(
        bwd_kernel,
        grid=(pairs,),
        in_specs=[first, second, first, first],
        out_specs=[pl.BlockSpec((rows, 2 * D), lambda pair: (0, 0)), first],
        out_shape=[
            jax.ShapeDtypeStruct((rows, 2 * D), LOW),
            jax.ShapeDtypeStruct((rows, D), LOW),
        ],
        scratch_shapes=[pltpu.VMEM((rows, 128), FLOAT), pltpu.VMEM((rows, 128), FLOAT)],
        compiler_params=pltpu.CompilerParams(vmem_limit_bytes=32 * 1024 * 1024),
        cost_estimate=pl.CostEstimate(
            flops=rows * rows * D, bytes_accessed=14 * rows * D, transcendentals=0
        ),
        name="attend_backward",
    )(qk, qk, values, grad)


def hop(value, axis, target):
    count = lax.axis_size(axis)
    return lax.ppermute(value, axis, [(source, target(source)) for source in range(count)])


def over_section(value):
    return hop(value, "section", lambda source: 1 - source)


def over_core(value):
    return hop(value, "shard", lambda source: source ^ 1)


def over_y(value):
    return hop(value, "shard", lambda source: source ^ 2)


def over_z(value, steps):
    count = lax.axis_size("shard")
    return hop(value, "shard", lambda source: (source + 4 * steps) % count)


def place(buffer, block, index, dim):
    starts = [0] * buffer.ndim
    starts[dim] = index
    return lax.dynamic_update_slice(buffer, block, starts)


def take(value, index, size, dim):
    return lax.dynamic_slice_in_dim(value, index * size, size, dim)


def place_of():
    shard = lax.axis_index("shard")
    return (lax.axis_index("section"), shard // 4, (shard // 2) % 2, shard % 2)


def spread_z(block):
    _, z, _, _ = place_of()
    count = lax.axis_size("shard") // 4
    buffer = jnp.zeros((count,) + block.shape, block.dtype)
    buffer = place(buffer, block[None], z, 0)
    for steps in range(1, count):
        arrived = over_z(block, steps)
        buffer = place(buffer, arrived[None], (z - steps) % count, 0)
    return buffer


def pair(own, arrived, index, dim):
    own, arrived = jnp.expand_dims(own, dim), jnp.expand_dims(arrived, dim)
    is_low = index == 0
    return jnp.concatenate(
        [jnp.where(is_low, own, arrived), jnp.where(is_low, arrived, own)], axis=dim
    )


def spread_y(blocks):
    _, _, y, _ = place_of()
    return pair(blocks, over_y(blocks), y, 1)


def spread_x(blocks):
    x, _, _, _ = place_of()
    return pair(blocks, over_section(blocks), x, blocks.ndim - 2)


def spread_core(blocks):
    _, _, _, core = place_of()
    return pair(blocks, over_core(blocks), core, 2)


def halves_of_both(shard):
    x, _, _, _ = place_of()
    half = shard.shape[0] // 2
    own = take(shard, x, half, 0)
    arrived = over_section(take(shard, 1 - x, half, 0))
    is_low = x == 0
    return (jnp.where(is_low, own, arrived), jnp.where(is_low, arrived, own))


def gather_vectors(packed):
    x, _, y, core = place_of()
    stacked = spread_z(packed)
    stacked = pair(stacked, over_y(stacked), y, 1)
    stacked = pair(stacked, over_core(stacked), core, 2)
    stacked = stacked.reshape((-1,) + packed.shape)
    arrived = over_section(stacked)
    return (jnp.where(x == 0, stacked, arrived), jnp.where(x == 0, arrived, stacked))


def reduce_pair(total, index, dim, exchange):
    sent = lax.dynamic_index_in_dim(total, 1 - index, dim, keepdims=False)
    kept = lax.dynamic_index_in_dim(total, index, dim, keepdims=False)
    return (kept.astype(FLOAT) + exchange(sent).astype(FLOAT)).astype(LOW)


def reduce_core(total):
    return reduce_pair(total, place_of()[3], 2, over_core)


def reduce_y(total):
    return reduce_pair(total, place_of()[2], 1, over_y)


def reduce_x(total):
    return reduce_pair(total, place_of()[0], total.ndim - 3, over_section)


def reduce_z(total):
    _, z, _, _ = place_of()
    count = total.shape[0]
    result = lax.dynamic_index_in_dim(total, z, 0, keepdims=False).astype(FLOAT)
    for steps in range(1, count):
        sent = lax.dynamic_index_in_dim(total, (z + steps) % count, 0, keepdims=False)
        result = result + over_z(sent, steps).astype(FLOAT)
    return result


def join_halves(first_layer, second_layer):
    x, _, _, _ = place_of()
    is_low = x == 0
    kept = jnp.where(is_low, first_layer, second_layer)
    arrived = over_section(jnp.where(is_low, second_layer, first_layer).astype(LOW)).astype(FLOAT)
    return jnp.concatenate(
        [jnp.where(is_low, kept, arrived), jnp.where(is_low, arrived, kept)], axis=0
    )


def scatter_vectors(first_layer, second_layer):
    x, z, y, core = place_of()
    count = lax.axis_size("shard")
    is_low = x == 0
    kept = jnp.where(is_low, first_layer, second_layer)
    total = kept + over_section(jnp.where(is_low, second_layer, first_layer))
    total = total.reshape((count // 4, 2, 2) + total.shape[1:])
    sent = lax.dynamic_index_in_dim(total, 1 - core, 2, keepdims=False)
    total = lax.dynamic_index_in_dim(total, core, 2, keepdims=False) + over_core(sent)
    sent = lax.dynamic_index_in_dim(total, 1 - y, 1, keepdims=False)
    total = lax.dynamic_index_in_dim(total, y, 1, keepdims=False) + over_y(sent)
    return reduce_z(total)


def unpack_vectors(stacked):
    rows = stacked.shape[0]
    singles = [stacked[:, item].reshape(-1) for item in range(6)]
    return singles + [stacked[:, 6:8].reshape(-1), stacked[:, 8:12].reshape(-1)]


def pack_vectors(singles, pair_vector, quad_vector, count):
    parts = [item.reshape(count, 1, -1) for item in singles]
    parts.append(pair_vector.reshape(count, 2, -1))
    parts.append(quad_vector.reshape(count, 4, -1))
    return jnp.concatenate(parts, axis=1)


def plain_gathered(shard):
    own = lax.all_gather(shard, "shard", axis=0, tiled=True)
    arrived = over_section(own)
    is_low = lax.axis_index("section") == 0
    return (jnp.where(is_low, own, arrived), jnp.where(is_low, arrived, own))


def plain_reduced(first, second):
    is_low = lax.axis_index("section") == 0
    kept = jnp.where(is_low, first, second).astype(FLOAT)
    arrived = over_section(jnp.where(is_low, second, first)).astype(FLOAT)
    return lax.psum_scatter(kept + arrived, "shard", scatter_dimension=0, tiled=True)


def forward_attention(hidden, qk, vo, vectors):
    ln1_gain, ln1_bias, out_bias, ln2_gain, ln2_bias, _, qv_bias, _ = [
        item.astype(FLOAT) for item in vectors
    ]
    h_float = hidden.astype(FLOAT)
    normed = norm_affine(h_float, ln1_gain, ln1_bias).astype(LOW)
    key_bias = jnp.concatenate([qv_bias[:D], jnp.zeros((D,), FLOAT)])
    qk_rows = (jnp.dot(normed, qk, preferred_element_type=FLOAT) + key_bias).astype(LOW)
    value_rows = (
        jnp.dot(normed, vo[:, :D], preferred_element_type=FLOAT) + qv_bias[D:]
    ).astype(LOW)
    attended = attention_forward(qk_rows, value_rows)
    residual = h_float + jnp.dot(attended, vo[:, D:], preferred_element_type=FLOAT) + out_bias
    normed_two = norm_affine(residual, ln2_gain, ln2_bias).astype(LOW)
    return (normed, qk_rows, value_rows, attended, residual, normed_two)


def forward_mlp(residual, normed_two, up, down, vectors):
    before = jnp.dot(normed_two, up, preferred_element_type=FLOAT) + vectors[7].astype(FLOAT)
    activated = jax.nn.gelu(before).astype(LOW)
    layer_out = (
        residual
        + jnp.dot(activated, down, preferred_element_type=FLOAT)
        + vectors[5].astype(FLOAT)
    )
    return (before, activated, layer_out)


def backward_mlp(grad_out, before, activated, normed_two, up, down):
    down_bias_grad = jnp.sum(grad_out, axis=0)
    grad_low = grad_out.astype(LOW)
    down_grad = dot_tn(activated, grad_low).astype(LOW)
    grad_act = dot_nt(grad_low, down)
    _, gelu_back = jax.vjp(jax.nn.gelu, before)
    (grad_before,) = gelu_back(grad_act)
    up_bias_grad = jnp.sum(grad_before, axis=0)
    before_low = grad_before.astype(LOW)
    up_grad = dot_tn(normed_two, before_low).astype(LOW)
    grad_normed = dot_nt(before_low, up)
    return (up_grad, down_grad, grad_normed, down_bias_grad, up_bias_grad)


def backward_to_scores(grad_out, grad_normed, residual, attended, qk_rows, value_rows, vo, vectors):
    _, norm_back = jax.vjp(norm_affine, residual, vectors[3].astype(FLOAT), vectors[4].astype(FLOAT))
    grad_norm, gain_grad, bias_grad = norm_back(grad_normed)
    grad_residual = grad_out + grad_norm
    out_bias_grad = jnp.sum(grad_residual, axis=0)
    residual_low = grad_residual.astype(LOW)
    out_grad = dot_tn(attended, residual_low).astype(LOW)
    grad_attended = dot_nt(residual_low, vo[:, D:]).astype(LOW)
    grad_qk, grad_v = attention_backward(qk_rows, value_rows, grad_attended)
    return (grad_residual, out_grad, grad_qk, grad_v, gain_grad, bias_grad, out_bias_grad)


def backward_input(grad_residual, grad_qk, grad_v, hidden, qk, vo, vectors):
    qv_bias_grad = jnp.concatenate(
        [
            jnp.sum(grad_qk[:, :D].astype(FLOAT), axis=0),
            jnp.sum(grad_v.astype(FLOAT), axis=0),
        ]
    )
    grad_normed = dot_nt(grad_qk, qk) + dot_nt(grad_v, vo[:, :D])
    _, norm_back = jax.vjp(
        norm_affine, hidden.astype(FLOAT), vectors[0].astype(FLOAT), vectors[1].astype(FLOAT)
    )
    grad_norm, gain_grad, bias_grad = norm_back(grad_normed)
    return ((grad_residual + grad_norm).astype(LOW), gain_grad, bias_grad, qv_bias_grad)


def tie(*values):
    return lax.optimization_barrier(values)


def second_stage(stacked, x_last):
    return spread_y(stacked) if x_last else spread_x(stacked)


def third_stage(stacked, x_last):
    return spread_x(stacked) if x_last else spread_y(stacked)


def core_stage(stacked):
    stacked = spread_core(stacked)
    return stacked.reshape(-1, stacked.shape[-1])


def core_reduced(total):
    count = lax.axis_size("shard")
    return reduce_core(
        total.reshape(count // 4, 2, 2, 2, total.shape[0] // (2 * count), total.shape[1])
    )


def wide_reduced(total, x_last):
    return reduce_x(total) if x_last else reduce_y(total)


def narrow_reduced(total, x_last):
    return reduce_y(total) if x_last else reduce_x(total)


def whole_gathered(main, down):
    columns = main.shape[1] // 4
    groups = [main[:, columns * item : columns * (item + 1)] for item in range(4)]
    packed = jnp.concatenate([jnp.concatenate(groups, axis=0), down], axis=1)
    return lax.all_gather(packed, ("shard", "section"), axis=0, tiled=True)


def parts_of(whole, devices):
    columns = whole.shape[1] - D
    main = whole[:, :columns].reshape(devices, 4, -1, columns)
    qk, vo, up_low, up_high = [main[:, item].reshape(-1, columns) for item in range(4)]
    return (qk, vo, jnp.concatenate([up_low, up_high], axis=1), whole[:, columns:])


def mlp_packed(up_grad, down_grad):
    count = lax.axis_size("shard")
    rows = D // (2 * count)
    blocks = down_grad.reshape(2 * count, -1, rows, D).transpose(0, 2, 1, 3)
    return jnp.concatenate([up_grad, blocks.reshape(D, -1)], axis=1)


def mlp_scattered(total, columns):
    rows = D // (2 * lax.axis_size("shard"))
    total = lax.psum_scatter(total, ("shard", "section"), scatter_dimension=0, tiled=True)
    total = total.astype(FLOAT)
    down = total[:, columns:].reshape(rows, -1, D).transpose(1, 0, 2).reshape(-1, D)
    return (total[:, :columns], down)


def on_device(
    boundary,
    ln1_gain,
    ln1_bias,
    w_qkv,
    qv_bias,
    w_out,
    out_bias,
    ln2_gain,
    ln2_bias,
    w_up,
    up_bias,
    w_down,
    down_bias,
):
    x = lax.axis_index("section")
    is_first = x == 0
    count = lax.axis_size("shard")
    direct = count <= 16
    cut = 4 * D
    packed = pack_vectors(
        [ln1_gain, ln1_bias, out_bias, ln2_gain, ln2_bias, down_bias], qv_bias, up_bias, 1
    )[0]
    main_shard = jnp.concatenate([w_qkv[0], w_out[0], w_up[0]], axis=1)
    traded = jnp.where(is_first, boundary[0, 1], boundary[0, 0])

    if direct:
        main0, main1 = halves_of_both(main_shard)
        down0, down1 = halves_of_both(w_down[0])
        main0, main1, down0, down1, packed, traded = tie(
            main0, main1, down0, down1, packed, traded
        )
        whole1 = whole_gathered(main1, down1)
        first_part, up0 = main0[:, :cut], main0[:, cut:]
        first_part = spread_z(first_part)
        vectors = gather_vectors(packed)
        other = over_section(traded)
        first_part, up0, down0, other = tie(first_part, up0, down0, other)
        qk0 = second_stage(first_part[..., : 2 * D], True)
        vo0 = second_stage(first_part[..., 2 * D :], False)
        up0 = spread_z(up0)
        qk0, vo0, up0, down0 = tie(qk0, vo0, up0, down0)
        qk0, vo0 = third_stage(qk0, True), third_stage(vo0, False)
        down0 = spread_z(down0)
        qk0, vo0, up0, down0 = tie(qk0, vo0, up0, down0)
        qk0, vo0 = core_stage(qk0), core_stage(vo0)
        up0, down0 = second_stage(up0, True), second_stage(down0, False)
        qk0, vo0, up0, down0 = tie(qk0, vo0, up0, down0)
    else:
        vectors = gather_vectors(packed)
        other = over_section(traded)
        main0, main1 = plain_gathered(main_shard)
        down0, down1 = plain_gathered(w_down[0])
        qk0, vo0, up0 = main0[:, : 2 * D], main0[:, 2 * D : cut], main0[:, cut:]
    vector0, vector1 = [unpack_vectors(item) for item in vectors]
    hidden = jnp.where(is_first, boundary[0, 0], other)
    cotangent = jnp.where(is_first, other, boundary[0, 1]).astype(FLOAT)

    kept0 = forward_attention(hidden, qk0, vo0, vector0)
    if direct:
        up0, down0 = third_stage(up0, True), third_stage(down0, False)
        kept0, up0, down0 = tie(kept0, up0, down0)
        up0, down0 = core_stage(up0), core_stage(down0)
    before0, activated0, out0 = forward_mlp(kept0[4], kept0[5], up0, down0, vector0)
    first_low = out0.astype(LOW)
    if direct:
        first_low, whole1 = tie(first_low, whole1)
        qk1, vo1, up1, down1 = parts_of(whole1, 2 * count)
    else:
        qk1, vo1, up1 = main1[:, : 2 * D], main1[:, 2 * D : cut], main1[:, cut:]
    kept1 = forward_attention(first_low, qk1, vo1, vector1)
    before1, activated1, out1 = forward_mlp(kept1[4], kept1[5], up1, down1, vector1)
    second_low = out1.astype(LOW)
    sent_out = jnp.where(is_first, second_low, first_low)
    if direct:
        sent_out, before1, activated1, cotangent = tie(sent_out, before1, activated1, cotangent)
    arrived_out = over_section(sent_out)
    mlp1 = backward_mlp(cotangent, before1, activated1, kept1[5], up1, down1)
    if direct:
        mlp1, arrived_out = tie(mlp1, arrived_out)
    up_grad1, down_grad1, grad_normed1, down_bias1, up_bias1 = mlp1
    back1 = backward_to_scores(
        cotangent, grad_normed1, kept1[4], kept1[3], kept1[1], kept1[2], vo1, vector1
    )
    residual1, out_grad1, grad_qk1, grad_v1, ln2_gain1, ln2_bias1, out_bias1 = back1
    mid_low, ln1_gain1, ln1_bias1, qv_bias1 = backward_input(
        residual1, grad_qk1, grad_v1, first_low, qk1, vo1, vector1
    )
    part_grad1 = jnp.concatenate(
        [
            dot_tn(kept1[0], grad_qk1).astype(LOW),
            dot_tn(kept1[0], grad_v1).astype(LOW),
            out_grad1,
        ],
        axis=1,
    )
    small1 = pack_vectors(
        [ln1_gain1, ln1_bias1, out_bias1, ln2_gain1, ln2_bias1, down_bias1], qv_bias1, up_bias1, count
    )
    if direct:
        up_sum1, down_sum1 = core_reduced(up_grad1), core_reduced(down_grad1)
        mid_low, part_grad1, small1, up_sum1, down_sum1 = tie(
            mid_low, part_grad1, small1, up_sum1, down_sum1
        )
        up_sum1, down_sum1 = wide_reduced(up_sum1, True), wide_reduced(down_sum1, False)
        part_sum1 = core_reduced(part_grad1)
    mid_float = mid_low.astype(FLOAT)
    mlp0 = backward_mlp(mid_float, before0, activated0, kept0[5], up0, down0)
    if direct:
        total0 = mlp_packed(mlp0[0], mlp0[1])
        mlp0, total0, up_sum1, down_sum1, part_sum1, mid_float = tie(
            mlp0, total0, up_sum1, down_sum1, part_sum1, mid_float
        )
        up_sum0, down_sum0 = mlp_scattered(total0, 4 * D)
    up_grad0, down_grad0, grad_normed0, down_bias0, up_bias0 = mlp0
    back0 = backward_to_scores(
        mid_float, grad_normed0, kept0[4], kept0[3], kept0[1], kept0[2], vo0, vector0
    )
    if direct:
        up_sum1, down_sum1 = narrow_reduced(up_sum1, True), narrow_reduced(down_sum1, False)
        qk_sum1 = wide_reduced(part_sum1[..., : 2 * D], True)
        vo_sum1 = wide_reduced(part_sum1[..., 2 * D :], False)
        back0, qk_sum1, vo_sum1, up_sum1, down_sum1 = tie(
            back0, qk_sum1, vo_sum1, up_sum1, down_sum1
        )
    residual0, out_grad0, grad_qk0, grad_v0, ln2_gain0, ln2_bias0, out_bias0 = back0
    part_grad0 = jnp.concatenate(
        [
            dot_tn(kept0[0], grad_qk0).astype(LOW),
            dot_tn(kept0[0], grad_v0).astype(LOW),
            out_grad0,
        ],
        axis=1,
    )
    if direct:
        part_sum1 = jnp.concatenate(
            [narrow_reduced(qk_sum1, True), narrow_reduced(vo_sum1, False)], axis=-1
        )
        up_sum1, down_sum1 = reduce_z(up_sum1), reduce_z(down_sum1)
        part_grad0, residual0, grad_qk0, grad_v0 = tie(part_grad0, residual0, grad_qk0, grad_v0)
        part_sum0 = core_reduced(part_grad0)
    in_low, ln1_gain0, ln1_bias0, qv_bias0 = backward_input(
        residual0, grad_qk0, grad_v0, hidden, qk0, vo0, vector0
    )
    small0 = pack_vectors(
        [ln1_gain0, ln1_bias0, out_bias0, ln2_gain0, ln2_bias0, down_bias0], qv_bias0, up_bias0, count
    )
    sent_grad = jnp.where(is_first, mid_low, in_low)
    if direct:
        part_sum1 = reduce_z(part_sum1)
        qk_sum0 = wide_reduced(part_sum0[..., : 2 * D], True)
        vo_sum0 = wide_reduced(part_sum0[..., 2 * D :], False)
        part_sum0 = jnp.concatenate(
            [narrow_reduced(qk_sum0, True), narrow_reduced(vo_sum0, False)], axis=-1
        )
        vector = scatter_vectors(small0, small1)
        arrived_grad = over_section(sent_grad)
        up, down = join_halves(up_sum0, up_sum1), join_halves(down_sum0, down_sum1)
        part = join_halves(reduce_z(part_sum0), part_sum1)
    else:
        arrived_grad = over_section(sent_grad)
        vector = scatter_vectors(small0, small1)
        part = plain_reduced(part_grad0, part_grad1)
        up, down = plain_reduced(up_grad0, up_grad1), plain_reduced(down_grad0, down_grad1)
    own_out = jnp.where(is_first, first_low, second_low)
    own_grad = jnp.where(is_first, in_low, mid_low)
    section_outputs = jnp.where(
        is_first, jnp.stack([own_out, arrived_out]), jnp.stack([arrived_out, own_out])
    )[None]
    section_grads = jnp.where(
        is_first, jnp.stack([own_grad, arrived_grad]), jnp.stack([arrived_grad, own_grad])
    )[None]
    return (
        section_outputs,
        section_grads,
        vector[0:1],
        vector[1:2],
        part[:, : 3 * D][None],
        vector[6:8].reshape(1, -1),
        part[:, 3 * D :][None],
        vector[2:3],
        vector[3:4],
        vector[4:5],
        up[None],
        vector[8:12].reshape(1, -1),
        down[None],
        vector[5:6],
    )


def solution(mesh):
    placed = (
        P("section", None, "shard", None),
        P("section", "shard"),
        P("section", "shard"),
        P("section", "shard", None),
        P("section", "shard"),
        P("section", "shard", None),
        P("section", "shard"),
        P("section", "shard"),
        P("section", "shard"),
        P("section", "shard", None),
        P("section", "shard"),
        P("section", "shard", None),
        P("section", "shard"),
    )
    return jax.shard_map(
        on_device,
        mesh=mesh,
        in_specs=placed,
        out_specs=(
            P("section", None, "shard", None),
            P("section", None, "shard", None),
            P("section", "shard"),
            P("section", "shard"),
            P("section", "shard", None),
            P("section", "shard"),
            P("section", "shard", None),
            P("section", "shard"),
            P("section", "shard"),
            P("section", "shard"),
            P("section", "shard", None),
            P("section", "shard"),
            P("section", "shard", None),
            P("section", "shard"),
        ),
        check_vma=False,
    )
```

```python
import jax
import jax.numpy as jnp
from jax import lax
from jax.experimental import pallas as pl
from jax.experimental.pallas import tpu as pltpu
from jax.sharding import PartitionSpec as P

D = 768
LOW = jnp.bfloat16
FLOAT = jnp.float32
CHUNK = 256


def norm_affine(values, gain, bias):
    row_mean = jnp.mean(values, axis=-1, keepdims=True)
    centred = values - row_mean
    variance = jnp.mean(centred * centred, axis=-1, keepdims=True)
    return centred * lax.rsqrt(variance + 1e-05) * gain + bias


def dot_nt(a,b):
    return lax.dot_general(a,b,(((1,),(1,)),((),())),preferred_element_type=FLOAT)


def dot_nn(a,b):
    return lax.dot_general(a,b,(((1,),(0,)),((),())),preferred_element_type=FLOAT)


def dot_tn(a,b):
    return lax.dot_general(a,b,(((0,),(0,)),((),())),preferred_element_type=FLOAT)


def head_part(block, head):
    lane = lax.broadcasted_iota(jnp.int32, block.shape, 1)
    return jnp.where((lane >= 64) == (head == 1), block, jnp.zeros_like(block))


def probabilities(q_rows, k_rows, first):
    scores = dot_nt(q_rows, k_rows)
    row = lax.broadcasted_iota(jnp.int32, scores.shape, 0) + first
    col = lax.broadcasted_iota(jnp.int32, scores.shape, 1)
    scores = jnp.where(col <= row, scores, -1e30)
    top = jnp.max(scores, axis=-1, keepdims=True)
    exponent = jnp.exp(scores - top)
    return exponent * (1.0 / jnp.sum(exponent, axis=-1, keepdims=True))


def fwd_kernel(q_ref, k_ref, v_ref, o_ref):
    rows = q_ref.shape[0]
    k = k_ref[...]; v = v_ref[...]
    for first in range(0, rows, CHUNK):
        last = first + CHUNK
        q = q_ref[first:last, :] * LOW(0.125)
        total = None
        for head in range(2):
            p = probabilities(head_part(q, head), k[:last], first).astype(LOW)
            part = dot_nn(p, head_part(v[:last], head))
            total = part if total is None else total + part
        o_ref[first:last, :] = total.astype(LOW)


def attention_forward(qk, values):
    rows = qk.shape[0]
    pairs = D // 128
    first = pl.BlockSpec((rows, 128), lambda pair: (0, pair))
    second = pl.BlockSpec((rows, 128), lambda pair: (0, pair + pairs))
    return pl.pallas_call(
        fwd_kernel,
        grid=(pairs,),
        in_specs=[first, second, first],
        out_specs=first,
        out_shape=jax.ShapeDtypeStruct((rows, D), LOW),
        compiler_params=pltpu.CompilerParams(vmem_limit_bytes=32 * 1024 * 1024),
        cost_estimate=pl.CostEstimate(
            flops=rows * rows * D, bytes_accessed=8 * rows * D, transcendentals=0
        ),
        name="attend_forward",
    )(qk, qk, values)


def bwd_kernel(q_ref, k_ref, v_ref, g_ref, qk_out, v_out, dk_acc, dv_acc):
    rows = q_ref.shape[0]
    h = pl.program_id(0)
    k = k_ref[...]; v = v_ref[...]
    dk_acc[...] = jnp.zeros_like(dk_acc)
    dv_acc[...] = jnp.zeros_like(dv_acc)
    col = pl.multiple_of(h * 128, 128)
    for first in range(0, rows, CHUNK):
        last = first + CHUNK
        q = q_ref[first:last, :] * LOW(0.125)
        g = g_ref[first:last, :]
        dq = None
        for head in range(2):
            qh = head_part(q, head); gh = head_part(g, head)
            p = probabilities(qh, k[:last], first)
            dp = dot_nt(gh, v[:last])
            centre = jnp.sum(p * dp, axis=-1, keepdims=True)
            ds = (p * (dp - centre)).astype(LOW)
            part = dot_nn(ds, head_part(k[:last], head))
            dq = part if dq is None else dq + part
            dk_acc[:last, :] += dot_tn(ds, qh)
            dv_acc[:last, :] += dot_tn(p.astype(LOW), gh)
        qk_out[first:last, pl.ds(col, 128)] = (dq * 0.125).astype(LOW)
    qk_out[:, pl.ds(D + col, 128)] = dk_acc[...].astype(LOW)
    v_out[...] = dv_acc[...].astype(LOW)


def attention_backward(qk, values, grad):
    rows = qk.shape[0]
    pairs = D // 128
    first = pl.BlockSpec((rows, 128), lambda pair: (0, pair))
    second = pl.BlockSpec((rows, 128), lambda pair: (0, pair + pairs))
    return pl.pallas_call(
        bwd_kernel,
        grid=(pairs,),
        in_specs=[first, second, first, first],
        out_specs=[pl.BlockSpec((rows, 2 * D), lambda pair: (0, 0)), first],
        out_shape=[
            jax.ShapeDtypeStruct((rows, 2 * D), LOW),
            jax.ShapeDtypeStruct((rows, D), LOW),
        ],
        scratch_shapes=[pltpu.VMEM((rows, 128), FLOAT), pltpu.VMEM((rows, 128), FLOAT)],
        compiler_params=pltpu.CompilerParams(vmem_limit_bytes=32 * 1024 * 1024),
        cost_estimate=pl.CostEstimate(
            flops=rows * rows * D, bytes_accessed=14 * rows * D, transcendentals=0
        ),
        name="attend_backward",
    )(qk, qk, values, grad)


def hop(value, axis, target):
    count = lax.axis_size(axis)
    return lax.ppermute(value, axis, [(source, target(source)) for source in range(count)])


def over_section(value):
    return hop(value, "section", lambda source: 1 - source)


def over_core(value):
    return hop(value, "shard", lambda source: source ^ 1)


def over_y(value):
    return hop(value, "shard", lambda source: source ^ 2)


def over_z(value, steps):
    count = lax.axis_size("shard")
    return hop(value, "shard", lambda source: (source + 4 * steps) % count)


def place(buffer, block, index, dim):
    starts = [0] * buffer.ndim
    starts[dim] = index
    return lax.dynamic_update_slice(buffer, block, starts)


def take(value, index, size, dim):
    return lax.dynamic_slice_in_dim(value, index * size, size, dim)


def place_of():
    shard = lax.axis_index("shard")
    return (lax.axis_index("section"), shard // 4, (shard // 2) % 2, shard % 2)


def spread_z(block):
    _, z, _, _ = place_of()
    count = lax.axis_size("shard") // 4
    buffer = jnp.zeros((count,) + block.shape, block.dtype)
    buffer = place(buffer, block[None], z, 0)
    for steps in range(1, count):
        arrived = over_z(block, steps)
        buffer = place(buffer, arrived[None], (z - steps) % count, 0)
    return buffer


def pair(own, arrived, index, dim):
    own, arrived = jnp.expand_dims(own, dim), jnp.expand_dims(arrived, dim)
    is_low = index == 0
    return jnp.concatenate(
        [jnp.where(is_low, own, arrived), jnp.where(is_low, arrived, own)], axis=dim
    )


def spread_y(blocks):
    _, _, y, _ = place_of()
    return pair(blocks, over_y(blocks), y, 1)


def spread_x(blocks):
    x, _, _, _ = place_of()
    return pair(blocks, over_section(blocks), x, blocks.ndim - 2)


def spread_core(blocks):
    _, _, _, core = place_of()
    return pair(blocks, over_core(blocks), core, 2)


def halves_of_both(shard):
    x, _, _, _ = place_of()
    half = shard.shape[0] // 2
    own = take(shard, x, half, 0)
    arrived = over_section(take(shard, 1 - x, half, 0))
    is_low = x == 0
    return (jnp.where(is_low, own, arrived), jnp.where(is_low, arrived, own))


def gather_vectors(packed):
    x, _, y, core = place_of()
    stacked = spread_z(packed)
    stacked = pair(stacked, over_y(stacked), y, 1)
    stacked = pair(stacked, over_core(stacked), core, 2)
    stacked = stacked.reshape((-1,) + packed.shape)
    arrived = over_section(stacked)
    return (jnp.where(x == 0, stacked, arrived), jnp.where(x == 0, arrived, stacked))


def reduce_pair(total, index, dim, exchange):
    sent = lax.dynamic_index_in_dim(total, 1 - index, dim, keepdims=False)
    kept = lax.dynamic_index_in_dim(total, index, dim, keepdims=False)
    return (kept.astype(FLOAT) + exchange(sent).astype(FLOAT)).astype(LOW)


def reduce_core(total):
    return reduce_pair(total, place_of()[3], 2, over_core)


def reduce_y(total):
    return reduce_pair(total, place_of()[2], 1, over_y)


def reduce_x(total):
    return reduce_pair(total, place_of()[0], total.ndim - 3, over_section)


def reduce_z(total):
    _, z, _, _ = place_of()
    count = total.shape[0]
    result = lax.dynamic_index_in_dim(total, z, 0, keepdims=False).astype(FLOAT)
    for steps in range(1, count):
        sent = lax.dynamic_index_in_dim(total, (z + steps) % count, 0, keepdims=False)
        result = result + over_z(sent, steps).astype(FLOAT)
    return result


def join_halves(first_layer, second_layer):
    x, _, _, _ = place_of()
    is_low = x == 0
    kept = jnp.where(is_low, first_layer, second_layer)
    arrived = over_section(jnp.where(is_low, second_layer, first_layer).astype(LOW)).astype(FLOAT)
    return jnp.concatenate(
        [jnp.where(is_low, kept, arrived), jnp.where(is_low, arrived, kept)], axis=0
    )


def scatter_vectors(first_layer, second_layer):
    x, z, y, core = place_of()
    count = lax.axis_size("shard")
    is_low = x == 0
    kept = jnp.where(is_low, first_layer, second_layer)
    total = kept + over_section(jnp.where(is_low, second_layer, first_layer))
    total = total.reshape((count // 4, 2, 2) + total.shape[1:])
    sent = lax.dynamic_index_in_dim(total, 1 - core, 2, keepdims=False)
    total = lax.dynamic_index_in_dim(total, core, 2, keepdims=False) + over_core(sent)
    sent = lax.dynamic_index_in_dim(total, 1 - y, 1, keepdims=False)
    total = lax.dynamic_index_in_dim(total, y, 1, keepdims=False) + over_y(sent)
    return reduce_z(total)


def unpack_vectors(stacked):
    rows = stacked.shape[0]
    singles = [stacked[:, item].reshape(-1) for item in range(6)]
    return singles + [stacked[:, 6:8].reshape(-1), stacked[:, 8:12].reshape(-1)]


def pack_vectors(singles, pair_vector, quad_vector, count):
    parts = [item.reshape(count, 1, -1) for item in singles]
    parts.append(pair_vector.reshape(count, 2, -1))
    parts.append(quad_vector.reshape(count, 4, -1))
    return jnp.concatenate(parts, axis=1)


def plain_gathered(shard):
    own = lax.all_gather(shard, "shard", axis=0, tiled=True)
    arrived = over_section(own)
    is_low = lax.axis_index("section") == 0
    return (jnp.where(is_low, own, arrived), jnp.where(is_low, arrived, own))


def plain_reduced(first, second):
    is_low = lax.axis_index("section") == 0
    kept = jnp.where(is_low, first, second).astype(FLOAT)
    arrived = over_section(jnp.where(is_low, second, first)).astype(FLOAT)
    return lax.psum_scatter(kept + arrived, "shard", scatter_dimension=0, tiled=True)


def forward_attention(hidden, qk, vo, vectors):
    ln1_gain, ln1_bias, out_bias, ln2_gain, ln2_bias, _, qv_bias, _ = [
        item.astype(FLOAT) for item in vectors
    ]
    h_float = hidden.astype(FLOAT)
    normed = norm_affine(h_float, ln1_gain, ln1_bias).astype(LOW)
    key_bias = jnp.concatenate([qv_bias[:D], jnp.zeros((D,), FLOAT)])
    qk_rows = (jnp.dot(normed, qk, preferred_element_type=FLOAT) + key_bias).astype(LOW)
    value_rows = (
        jnp.dot(normed, vo[:, :D], preferred_element_type=FLOAT) + qv_bias[D:]
    ).astype(LOW)
    attended = attention_forward(qk_rows, value_rows)
    residual = h_float + jnp.dot(attended, vo[:, D:], preferred_element_type=FLOAT) + out_bias
    normed_two = norm_affine(residual, ln2_gain, ln2_bias).astype(LOW)
    return (normed, qk_rows, value_rows, attended, residual, normed_two)


def forward_mlp(residual, normed_two, up, down, vectors):
    before = jnp.dot(normed_two, up, preferred_element_type=FLOAT) + vectors[7].astype(FLOAT)
    activated = jax.nn.gelu(before).astype(LOW)
    layer_out = (
        residual
        + jnp.dot(activated, down, preferred_element_type=FLOAT)
        + vectors[5].astype(FLOAT)
    )
    return (before, activated, layer_out)


def backward_mlp(grad_out, before, activated, normed_two, up, down):
    down_bias_grad = jnp.sum(grad_out, axis=0)
    grad_low = grad_out.astype(LOW)
    down_grad = dot_tn(activated, grad_low).astype(LOW)
    grad_act = dot_nt(grad_low, down)
    _, gelu_back = jax.vjp(jax.nn.gelu, before)
    (grad_before,) = gelu_back(grad_act)
    up_bias_grad = jnp.sum(grad_before, axis=0)
    before_low = grad_before.astype(LOW)
    up_grad = dot_tn(normed_two, before_low).astype(LOW)
    grad_normed = dot_nt(before_low, up)
    return (up_grad, down_grad, grad_normed, down_bias_grad, up_bias_grad)


def backward_to_scores(grad_out, grad_normed, residual, attended, qk_rows, value_rows, vo, vectors):
    _, norm_back = jax.vjp(norm_affine, residual, vectors[3].astype(FLOAT), vectors[4].astype(FLOAT))
    grad_norm, gain_grad, bias_grad = norm_back(grad_normed)
    grad_residual = grad_out + grad_norm
    out_bias_grad = jnp.sum(grad_residual, axis=0)
    residual_low = grad_residual.astype(LOW)
    out_grad = dot_tn(attended, residual_low).astype(LOW)
    grad_attended = dot_nt(residual_low, vo[:, D:]).astype(LOW)
    grad_qk, grad_v = attention_backward(qk_rows, value_rows, grad_attended)
    return (grad_residual, out_grad, grad_qk, grad_v, gain_grad, bias_grad, out_bias_grad)


def backward_input(grad_residual, grad_qk, grad_v, hidden, qk, vo, vectors):
    qv_bias_grad = jnp.concatenate(
        [
            jnp.sum(grad_qk[:, :D].astype(FLOAT), axis=0),
            jnp.sum(grad_v.astype(FLOAT), axis=0),
        ]
    )
    grad_normed = dot_nt(grad_qk, qk) + dot_nt(grad_v, vo[:, :D])
    _, norm_back = jax.vjp(
        norm_affine, hidden.astype(FLOAT), vectors[0].astype(FLOAT), vectors[1].astype(FLOAT)
    )
    grad_norm, gain_grad, bias_grad = norm_back(grad_normed)
    return ((grad_residual + grad_norm).astype(LOW), gain_grad, bias_grad, qv_bias_grad)


def tie(*values):
    return lax.optimization_barrier(values)


def second_stage(stacked, x_last):
    return spread_y(stacked) if x_last else spread_x(stacked)


def third_stage(stacked, x_last):
    return spread_x(stacked) if x_last else spread_y(stacked)


def core_stage(stacked):
    stacked = spread_core(stacked)
    return stacked.reshape(-1, stacked.shape[-1])


def core_reduced(total):
    count = lax.axis_size("shard")
    return reduce_core(
        total.reshape(count // 4, 2, 2, 2, total.shape[0] // (2 * count), total.shape[1])
    )


def wide_reduced(total, x_last):
    return reduce_x(total) if x_last else reduce_y(total)


def narrow_reduced(total, x_last):
    return reduce_y(total) if x_last else reduce_x(total)


def whole_gathered(main, down):
    columns = main.shape[1] // 4
    groups = [main[:, columns * item : columns * (item + 1)] for item in range(4)]
    packed = jnp.concatenate([jnp.concatenate(groups, axis=0), down], axis=1)
    return lax.all_gather(packed, ("shard", "section"), axis=0, tiled=True)


def parts_of(whole, devices):
    columns = whole.shape[1] - D
    main = whole[:, :columns].reshape(devices, 4, -1, columns)
    qk, vo, up_low, up_high = [main[:, item].reshape(-1, columns) for item in range(4)]
    return (qk, vo, jnp.concatenate([up_low, up_high], axis=1), whole[:, columns:])


def mlp_packed(up_grad, down_grad):
    count = lax.axis_size("shard")
    rows = D // (2 * count)
    blocks = down_grad.reshape(2 * count, -1, rows, D).transpose(0, 2, 1, 3)
    return jnp.concatenate([up_grad, blocks.reshape(D, -1)], axis=1)


def mlp_scattered(total, columns):
    rows = D // (2 * lax.axis_size("shard"))
    total = lax.psum_scatter(total, ("shard", "section"), scatter_dimension=0, tiled=True)
    total = total.astype(FLOAT)
    down = total[:, columns:].reshape(rows, -1, D).transpose(1, 0, 2).reshape(-1, D)
    return (total[:, :columns], down)


def on_device(
    boundary,
    ln1_gain,
    ln1_bias,
    w_qkv,
    qv_bias,
    w_out,
    out_bias,
    ln2_gain,
    ln2_bias,
    w_up,
    up_bias,
    w_down,
    down_bias,
):
    x = lax.axis_index("section")
    is_first = x == 0
    count = lax.axis_size("shard")
    direct = count <= 16
    cut = 4 * D
    packed = pack_vectors(
        [ln1_gain, ln1_bias, out_bias, ln2_gain, ln2_bias, down_bias], qv_bias, up_bias, 1
    )[0]
    main_shard = jnp.concatenate([w_qkv[0], w_out[0], w_up[0]], axis=1)
    traded = jnp.where(is_first, boundary[0, 1], boundary[0, 0])

    if direct:
        main0, main1 = halves_of_both(main_shard)
        down0, down1 = halves_of_both(w_down[0])
        main0, main1, down0, down1, packed, traded = tie(
            main0, main1, down0, down1, packed, traded
        )
        whole1 = whole_gathered(main1, down1)
        first_part, up0 = main0[:, :cut], main0[:, cut:]
        first_part = spread_z(first_part)
        vectors = gather_vectors(packed)
        other = over_section(traded)
        first_part, up0, down0, other = tie(first_part, up0, down0, other)
        qk0 = second_stage(first_part[..., : 2 * D], True)
        vo0 = second_stage(first_part[..., 2 * D :], False)
        up0 = spread_z(up0)
        qk0, vo0, up0, down0 = tie(qk0, vo0, up0, down0)
        qk0, vo0 = third_stage(qk0, True), third_stage(vo0, False)
        down0 = spread_z(down0)
        qk0, vo0, up0, down0 = tie(qk0, vo0, up0, down0)
        qk0, vo0 = core_stage(qk0), core_stage(vo0)
        up0, down0 = second_stage(up0, True), second_stage(down0, False)
        qk0, vo0, up0, down0 = tie(qk0, vo0, up0, down0)
    else:
        vectors = gather_vectors(packed)
        other = over_section(traded)
        main0, main1 = plain_gathered(main_shard)
        down0, down1 = plain_gathered(w_down[0])
        qk0, vo0, up0 = main0[:, : 2 * D], main0[:, 2 * D : cut], main0[:, cut:]
    vector0, vector1 = [unpack_vectors(item) for item in vectors]
    hidden = jnp.where(is_first, boundary[0, 0], other)
    cotangent = jnp.where(is_first, other, boundary[0, 1]).astype(FLOAT)

    kept0 = forward_attention(hidden, qk0, vo0, vector0)
    if direct:
        up0, down0 = third_stage(up0, True), third_stage(down0, False)
        kept0, up0, down0 = tie(kept0, up0, down0)
        up0, down0 = core_stage(up0), core_stage(down0)
    before0, activated0, out0 = forward_mlp(kept0[4], kept0[5], up0, down0, vector0)
    first_low = out0.astype(LOW)
    if direct:
        first_low, whole1 = tie(first_low, whole1)
        qk1, vo1, up1, down1 = parts_of(whole1, 2 * count)
    else:
        qk1, vo1, up1 = main1[:, : 2 * D], main1[:, 2 * D : cut], main1[:, cut:]
    kept1 = forward_attention(first_low, qk1, vo1, vector1)
    before1, activated1, out1 = forward_mlp(kept1[4], kept1[5], up1, down1, vector1)
    second_low = out1.astype(LOW)
    sent_out = jnp.where(is_first, second_low, first_low)
    if direct:
        sent_out, before1, activated1, cotangent = tie(sent_out, before1, activated1, cotangent)
    arrived_out = over_section(sent_out)
    mlp1 = backward_mlp(cotangent, before1, activated1, kept1[5], up1, down1)
    if direct:
        mlp1 = tie(*mlp1)
    up_grad1, down_grad1, grad_normed1, down_bias1, up_bias1 = mlp1
    back1 = backward_to_scores(
        cotangent, grad_normed1, kept1[4], kept1[3], kept1[1], kept1[2], vo1, vector1
    )
    residual1, out_grad1, grad_qk1, grad_v1, ln2_gain1, ln2_bias1, out_bias1 = back1
    mid_low, ln1_gain1, ln1_bias1, qv_bias1 = backward_input(
        residual1, grad_qk1, grad_v1, first_low, qk1, vo1, vector1
    )
    part_grad1 = jnp.concatenate(
        [
            dot_tn(kept1[0], grad_qk1).astype(LOW),
            dot_tn(kept1[0], grad_v1).astype(LOW),
            out_grad1,
        ],
        axis=1,
    )
    small1 = pack_vectors(
        [ln1_gain1, ln1_bias1, out_bias1, ln2_gain1, ln2_bias1, down_bias1], qv_bias1, up_bias1, count
    )
    if direct:
        up_sum1, down_sum1 = core_reduced(up_grad1), core_reduced(down_grad1)
        mid_low, part_grad1, small1, up_sum1, down_sum1, arrived_out = tie(
            mid_low, part_grad1, small1, up_sum1, down_sum1, arrived_out
        )
        up_sum1, down_sum1 = wide_reduced(up_sum1, True), wide_reduced(down_sum1, False)
        part_sum1 = core_reduced(part_grad1)
    mid_float = mid_low.astype(FLOAT)
    mlp0 = backward_mlp(mid_float, before0, activated0, kept0[5], up0, down0)
    if direct:
        total0 = mlp_packed(mlp0[0], mlp0[1])
        mlp0, total0, part_sum1, mid_float = tie(mlp0, total0, part_sum1, mid_float)
        up_sum0, down_sum0 = mlp_scattered(total0, 4 * D)
    up_grad0, down_grad0, grad_normed0, down_bias0, up_bias0 = mlp0
    back0 = backward_to_scores(
        mid_float, grad_normed0, kept0[4], kept0[3], kept0[1], kept0[2], vo0, vector0
    )
    if direct:
        up_sum1, down_sum1 = narrow_reduced(up_sum1, True), narrow_reduced(down_sum1, False)
        qk_sum1 = wide_reduced(part_sum1[..., : 2 * D], True)
        vo_sum1 = wide_reduced(part_sum1[..., 2 * D :], False)
        back0, qk_sum1, vo_sum1, up_sum1, down_sum1 = tie(
            back0, qk_sum1, vo_sum1, up_sum1, down_sum1
        )
    residual0, out_grad0, grad_qk0, grad_v0, ln2_gain0, ln2_bias0, out_bias0 = back0
    part_grad0 = jnp.concatenate(
        [
            dot_tn(kept0[0], grad_qk0).astype(LOW),
            dot_tn(kept0[0], grad_v0).astype(LOW),
            out_grad0,
        ],
        axis=1,
    )
    if direct:
        part_sum1 = jnp.concatenate(
            [narrow_reduced(qk_sum1, True), narrow_reduced(vo_sum1, False)], axis=-1
        )
        up_sum1, down_sum1 = reduce_z(up_sum1), reduce_z(down_sum1)
        part_grad0, residual0, grad_qk0, grad_v0 = tie(part_grad0, residual0, grad_qk0, grad_v0)
        part_sum0 = core_reduced(part_grad0)
    in_low, ln1_gain0, ln1_bias0, qv_bias0 = backward_input(
        residual0, grad_qk0, grad_v0, hidden, qk0, vo0, vector0
    )
    small0 = pack_vectors(
        [ln1_gain0, ln1_bias0, out_bias0, ln2_gain0, ln2_bias0, down_bias0], qv_bias0, up_bias0, count
    )
    sent_grad = jnp.where(is_first, mid_low, in_low)
    if direct:
        part_sum1 = reduce_z(part_sum1)
        qk_sum0 = wide_reduced(part_sum0[..., : 2 * D], True)
        vo_sum0 = wide_reduced(part_sum0[..., 2 * D :], False)
        part_sum0 = jnp.concatenate(
            [narrow_reduced(qk_sum0, True), narrow_reduced(vo_sum0, False)], axis=-1
        )
        vector = scatter_vectors(small0, small1)
        arrived_grad = over_section(sent_grad)
        up, down = join_halves(up_sum0, up_sum1), join_halves(down_sum0, down_sum1)
        part = join_halves(reduce_z(part_sum0), part_sum1)
    else:
        arrived_grad = over_section(sent_grad)
        vector = scatter_vectors(small0, small1)
        part = plain_reduced(part_grad0, part_grad1)
        up, down = plain_reduced(up_grad0, up_grad1), plain_reduced(down_grad0, down_grad1)
    own_out = jnp.where(is_first, first_low, second_low)
    own_grad = jnp.where(is_first, in_low, mid_low)
    section_outputs = jnp.where(
        is_first, jnp.stack([own_out, arrived_out]), jnp.stack([arrived_out, own_out])
    )[None]
    section_grads = jnp.where(
        is_first, jnp.stack([own_grad, arrived_grad]), jnp.stack([arrived_grad, own_grad])
    )[None]
    return (
        section_outputs,
        section_grads,
        vector[0:1],
        vector[1:2],
        part[:, : 3 * D][None],
        vector[6:8].reshape(1, -1),
        part[:, 3 * D :][None],
        vector[2:3],
        vector[3:4],
        vector[4:5],
        up[None],
        vector[8:12].reshape(1, -1),
        down[None],
        vector[5:6],
    )


def solution(mesh):
    placed = (
        P("section", None, "shard", None),
        P("section", "shard"),
        P("section", "shard"),
        P("section", "shard", None),
        P("section", "shard"),
        P("section", "shard", None),
        P("section", "shard"),
        P("section", "shard"),
        P("section", "shard"),
        P("section", "shard", None),
        P("section", "shard"),
        P("section", "shard", None),
        P("section", "shard"),
    )
    return jax.shard_map(
        on_device,
        mesh=mesh,
        in_specs=placed,
        out_specs=(
            P("section", None, "shard", None),
            P("section", None, "shard", None),
            P("section", "shard"),
            P("section", "shard"),
            P("section", "shard", None),
            P("section", "shard"),
            P("section", "shard", None),
            P("section", "shard"),
            P("section", "shard"),
            P("section", "shard"),
            P("section", "shard", None),
            P("section", "shard"),
            P("section", "shard", None),
            P("section", "shard"),
        ),
        check_vma=False,
    )
```
